128 devices in a mesh: lat: 8 (over z, core), lon: 16 (over x, y).
Axes of the slice: x: 4, y: 4, z: 4, core: 2. Of those that a mesh axis runs over, the one named last changes fastest.
Arguments:
- reading_values: bfloat16 [131072, 256], P(('lat', 'lon')), may hold values from -6 to 6
- reading_tile: int32 [131072, 1], P(('lat', 'lon')), may hold values from 0 to 15; in each aligned block of 1024 rows (0 to 1023, 1024 to 2047, ...) at most 128 rows name the same one
- reading_cell: int32 [131072], P(('lat', 'lon')), may hold values from 0 to 4095
- in_weight: bfloat16 [256, 512], P('lat'), may hold values from -0.75 to 0.75
- kernel: float32 [9, 512], replicated, may hold values from -2 to 2
- norm_gain: float32 [512], replicated, may hold values from 0.1 to 1.9
- mix_weight: bfloat16 [512, 512], P('lat'), may hold values from -0.25 to 0.25
Outputs:
- latent_grid: bfloat16 [512, 1024, 512], P('lat', 'lon')
The draws below stay inside these ranges and needn't reach their ends.
Inputs may be any that keep to these rules, and one draw needn't show every extreme that they name: `reading_tile`: among the 1024 readings of one device no tile is named by more than 128 of them, a bound that some block reaches.
All inputs are finite; a program needn't handle non-finite values.
Results may differ from the reference program's by a relative error of at most 0.014.
Values may be sent and summed in bfloat16 or wider, within the bound.
A program may use at most 64 MiB of HBM per device.

```python
import math
import jax
import jax.numpy as jnp
import numpy as np
from jax import lax

NCH = 256
LATENT = 512
LAT_DEV = 64
LON_DEV = 64
OBS_DEV = 1024
CAP = 128
READINGS = 131072
N_LAT = 8
N_LON = 16


def touch_ends(values, rng, smallest, top_value):
    shape = values.shape
    place = [jax.random.randint(jax.random.fold_in(rng, axis), (), 0, shape[axis]) for axis in range(len(shape))]
    values = values.at[tuple(place)].set(smallest)
    longest = shape.index(max(shape))
    place[longest] = (place[longest] + 1) % shape[longest]
    return values.at[tuple(place)].set(top_value)


def level_of(key, extent, split, least, top_value):
    def one(position, parts):
        heights = jax.random.uniform(jax.random.fold_in(jax.random.fold_in(key, 6), position), (parts,), jnp.float32, least / len(split), top_value / len(split))
        return jnp.repeat(jnp.exp(heights), extent[position] // parts).reshape((-1,) + (1,) * (len(extent) - position - 1))

    factor_of = one(*split[0])
    for cut in split[1:]:
        factor_of = factor_of * one(*cut)
    return factor_of


def deal_out(own_key, own, number, rows, number_of, top, bound, lean):
    order = jax.random.permutation(own_key, number_of)
    heavy_load, common = shares(number_of, rows * top, bound, lean, True), shares(number_of, rows * top, bound, lean, False)
    places = jnp.arange(number_of)

    def named(sizes, offset_by):
        used = int((sizes > 0).sum())
        fixed = max(1, used // 4)
        passed = fixed + (places - fixed + offset_by * (used - fixed)) % max(1, number_of - fixed)
        return jnp.zeros((number_of,), jnp.int32).at[order[jnp.where(places < fixed, places, passed)]].set(jnp.asarray(sizes, jnp.int32))

    sizes = jnp.where(number % 4 == 0, named(heavy_load, number // 4), named(common, number - number // 4 - 1))
    mixed = jax.random.permutation(jax.random.fold_in(own, 3), number_of)
    source_of, receiver = mixed[0:number_of // 2 * 2:2], mixed[1:number_of // 2 * 2:2]
    room = jnp.minimum(sizes[source_of] - 1, bound - sizes[receiver]) // 2
    room = jnp.where((source_of == order[0]) | (receiver == order[0]) | (sizes[receiver] == 0), 0, jnp.maximum(room, 0))
    passed = jax.random.randint(jax.random.fold_in(own, 4), (number_of // 2,), 0, 1 << 20) % (room + 1)
    sizes = sizes.at[source_of].add(-passed).at[receiver].add(passed)
    items = jnp.searchsorted(jnp.cumsum(sizes), jnp.arange(rows * top), side="right").astype(jnp.int32)
    table = items.reshape(top, rows).T
    table = table[jax.random.permutation(jax.random.fold_in(own, 1), rows)]
    offset_by = jax.random.randint(jax.random.fold_in(own, 2), (rows, 1), 0, top)
    return jnp.take_along_axis(table, (jnp.arange(top)[None, :] + offset_by) % top, axis=1)


def shares(count, total, bound, slope, full):
    loads = [(1 << 20) // math.isqrt(standing ** slope) + 1 for standing in range(1, count + 1)]
    largest = bound if full else min(bound, max(-(-total // count), total * loads[0] // sum(loads)))
    least = 1 if total - largest >= count - 1 else 0
    given, rest = [largest] + [least] * (count - 1), total - largest - least * (count - 1)
    while rest > 0:
        candidates = [i for i in range(1, count) if given[i] < largest] or [i for i in range(1, count) if given[i] < bound]
        mass, remaining = sum([loads[i] for i in candidates]), rest
        for i in candidates:
            more = min(bound - given[i], max(1, remaining * loads[i] // mass), rest)
            given[i] = given[i] + more
            rest = rest - more
    return np.array(given)


def normal_values(stream_key, extent, deviation, bound, pieces=(), kind=jnp.bfloat16):
    array = deviation * jax.random.normal(stream_key, extent, jnp.float32)
    if pieces:
        array = array * level_of(stream_key, extent, pieces, -0.22, 0.18)
    return jnp.clip(array, -bound, bound).astype(kind)


def setup_inputs(seed: int = 0) -> dict:
    arg_keys = jax.random.split(jax.random.key(seed), 8)
    reading_values = normal_values(arg_keys[0], (READINGS, NCH), 1.0, 6.0, ((0, 128),))
    reading_tile_keys = jax.random.split(jax.random.fold_in(arg_keys[1], 1), READINGS // OBS_DEV)
    reading_tile_turns = jax.random.permutation(jax.random.fold_in(arg_keys[1], 3), READINGS // OBS_DEV)
    reading_tile = jax.vmap(lambda own, number: deal_out(jax.random.fold_in(arg_keys[1], 2), own, number, OBS_DEV, N_LON, 1, CAP, 2))(reading_tile_keys, reading_tile_turns).reshape((READINGS, 1))
    reading_cell = touch_ends(jax.random.randint(arg_keys[2], (READINGS,), 0, LAT_DEV * LON_DEV), jax.random.fold_in(arg_keys[2], 1), 0, (LAT_DEV * LON_DEV) - 1).astype(jnp.int32)
    in_weight = normal_values(arg_keys[3], (NCH, LATENT), (NCH // 4) ** -0.5, 0.75, ((0, 8),))
    kernel = normal_values(arg_keys[4], (9, LATENT), 0.4, 2.0, (), jnp.float32)
    norm_gain = jnp.clip(1.0 + 0.18 * jax.random.normal(arg_keys[5], (LATENT,), jnp.float32), 0.1, 1.9)
    mix_weight = normal_values(arg_keys[6], (LATENT, LATENT), LATENT ** -0.5, 0.25, ((0, 8),))
    return {"reading_values": reading_values, "reading_tile": reading_tile, "reading_cell": reading_cell, "in_weight": in_weight, "kernel": kernel, "norm_gain": norm_gain, "mix_weight": mix_weight}


def setconv(values, cell_ids):
    cell_total = LAT_DEV * LON_DEV
    block_size = min(512, cell_total)
    live = cell_ids >= 0
    obs_row = (cell_ids // LON_DEV).astype(jnp.float32)
    obs_col = (cell_ids % LON_DEV).astype(jnp.float32)

    def one_block(block_start):
        cell_index = block_start + jnp.arange(block_size, dtype=jnp.int32)
        cell_row = (cell_index // LON_DEV).astype(jnp.float32)
        cell_col = (cell_index % LON_DEV).astype(jnp.float32)
        distance = (cell_row[:, None] - obs_row[None, :]) ** 2 + (cell_col[:, None] - obs_col[None, :]) ** 2
        inside = live[None, :] & (distance <= 36.0)
        weights = jnp.where(inside, jnp.exp(-distance / 36.0), 0.0).astype(jnp.bfloat16)
        density = lax.optimization_barrier(jnp.sum(weights.astype(jnp.float32), axis=1))
        encoded = jnp.dot(weights, values, preferred_element_type=jnp.float32)
        return (encoded / (density[:, None] + 1.0)).astype(jnp.bfloat16)
    starts = jnp.arange(cell_total // block_size, dtype=jnp.int32) * block_size
    return lax.map(one_block, starts).reshape(cell_total, values.shape[1])

def reference(reading_values, reading_tile, reading_cell, in_weight, kernel, norm_gain, mix_weight):
    band_rows = OBS_DEV * N_LON
    slot_count = 2 * OBS_DEV
    values = reading_values.reshape(N_LAT, band_rows, NCH)
    targets = reading_tile[:, 0].reshape(N_LAT, band_rows)
    cells = reading_cell.reshape(N_LAT, band_rows)

    def one_band(band):
        band_values, band_targets, band_cells = band

        def one_tile(tile):
            order = jnp.argsort(jnp.where(band_targets == tile, 0, 1).astype(jnp.int32), stable=True)[:slot_count]
            live = band_targets[order] == tile
            picked_cells = jnp.where(live, band_cells[order], -1).astype(jnp.int32)
            return setconv(band_values[order], picked_cells)
        return lax.map(one_tile, jnp.arange(N_LON, dtype=jnp.int32))
    grid = lax.map(one_band, (values, targets, cells))
    grid = grid.reshape(N_LAT, N_LON, LAT_DEV, LON_DEV, NCH).transpose(0, 2, 1, 3, 4)
    grid = grid.reshape(N_LAT * LAT_DEV * N_LON * LON_DEV, NCH)
    height = N_LAT * LAT_DEV
    width = N_LON * LON_DEV
    latent = jnp.dot(grid, in_weight, preferred_element_type=jnp.float32).astype(jnp.bfloat16)
    latent = latent.reshape(height, width, LATENT)
    padded = jnp.pad(latent, ((0, 0), (1, 1), (0, 0)), mode='wrap')
    padded = jnp.pad(padded, ((1, 1), (0, 0), (0, 0)))
    neighbours = jnp.zeros((height, width, LATENT), jnp.float32)
    for row_shift in range(3):
        for col_shift in range(3):
            neighbours = neighbours + kernel[3 * row_shift + col_shift] * padded[row_shift:row_shift + height, col_shift:col_shift + width].astype(jnp.float32)
    square_mean = lax.optimization_barrier(jnp.mean(neighbours * neighbours, axis=-1, keepdims=True))
    normed = (neighbours * lax.rsqrt(square_mean + 1e-06) * norm_gain).astype(jnp.bfloat16)
    mixed = jnp.dot(normed.reshape(height * width, LATENT), mix_weight, preferred_element_type=jnp.float32)
    result = latent.reshape(height * width, LATENT).astype(jnp.float32) + jax.nn.silu(mixed)
    return result.astype(jnp.bfloat16).reshape(height, width, LATENT)
```

```python
import jax
import jax.numpy as jnp
from jax import lax
from jax.experimental import pallas as pl
from jax.experimental.pallas import tpu as pltpu
from jax.sharding import PartitionSpec as P

F32 = jnp.float32
BF16 = jnp.bfloat16
MESH = pl.DeviceIdType.MESH

NCH = 256
LATENT = 512
SIDE = 64
OWN = 1024
CAP = 128
TILES = 16
BANDS = 8
GROUP = 4
GROUPS = TILES // GROUP
KDIM = GROUP * CAP
BLOCK_ROWS = 16
BLOCK = BLOCK_ROWS * SIDE
BLOCKS = SIDE // BLOCK_ROWS
CELLS = SIDE * SIDE
RINGS = ((6, 0, 0), (5, 1, 3), (4, 4, 4), (3, 5, 5), (0, 6, 6))


def iota(shape, dim):
    return lax.broadcasted_iota(jnp.int32, shape, dim)


def nt_dot(a, b):
    return lax.dot_general(a, b, (((1,), (1,)), ((), ())), preferred_element_type=F32)


def exact_dot(a, b):
    return jnp.dot(a, b, preferred_element_type=F32, precision=lax.Precision.HIGHEST)


def wide(row):
    return jnp.broadcast_to(row, (16, row.shape[1])).astype(BF16)


def encode_kernel(
    vals, tile, cell, inw, mixw,
    h_out, up, down, left, right, corners, mix_out,
    onehot, cmsg, crecv, sbuf, recv, in_full,
    near_r, near_c, gain_r, gain_c, room_r, room_c, er_f, ec_f,
    counts, recip, wbuf, acc, eacc, webuf, ebuf, cbuf, hbuf,
    v_send, v_recv, c_send, c_recv, i_send, i_recv, m_send, m_recv, e_send, e_recv, k_send, k_recv,
    h_sem, l_sem,
):
    lat = lax.axis_index("lat")
    lon = lax.axis_index("lon")
    east, west = (lon + 1) % TILES, (lon + TILES - 1) % TILES
    north, south = (lat + BANDS - 1) % BANDS, (lat + 1) % BANDS
    lon_x, lon_y = lon // 4, lon % 4

    def partner(k):
        return ((lon_x + k // 4) % 4) * 4 + (lon_y + k % 4) % 4

    barrier = pltpu.get_barrier_semaphore()

    def greet(where):
        pl.semaphore_signal(barrier, inc=1, device_id=where, device_id_type=MESH)

    for k in range(1, TILES):
        greet((lat, partner(k)))
    for d in range(1, BANDS):
        greet(((lat + d) % BANDS, lon))
    for a in (north, south):
        for b in (west, east):
            greet((a, b))

    tid = tile[...]
    belongs = (iota((TILES, OWN), 0) == tid).astype(F32)
    before = (iota((128, 128), 0) < iota((128, 128), 1)).astype(F32).astype(BF16)
    carry = jnp.zeros((TILES, 1), F32)
    ranks = []
    for b in range(OWN // 128):
        part = belongs[:, 128 * b : 128 * b + 128]
        within = jnp.dot(part.astype(BF16), before, preferred_element_type=F32)
        ranks.append(jnp.sum(part * (within + carry), axis=0, keepdims=True))
        carry = carry + jnp.sum(part, axis=1, keepdims=True)
    rank = jnp.concatenate(ranks, axis=1)
    onehot[...] = (iota((CAP, OWN), 0).astype(F32) == rank).astype(F32).astype(BF16)

    rows = (cell[...] >> 6).astype(F32) + 1.0
    cols = (cell[...] & 63).astype(F32) + 1.0
    line = iota((8 * TILES, OWN), 0)
    which = line & 7
    info = jnp.where(which == 0, rows, jnp.where(which == 1, cols, 0.0))
    info = jnp.where((line >> 3) == tid, info, 0.0).astype(BF16)
    cmsg[...] = nt_dot(info, onehot[...]).reshape(TILES, 8, CAP)
    crecv[0] = cmsg[lon]

    pl.semaphore_wait(barrier, TILES - 1 + BANDS - 1 + 4)

    def cell_copy(k):
        return pltpu.make_async_remote_copy(
            cmsg.at[partner(k)], crecv.at[k], c_send.at[k], c_recv.at[k],
            device_id=(lat, partner(k)), device_id_type=MESH)

    def value_copy(k):
        return pltpu.make_async_remote_copy(
            sbuf.at[k], recv.at[k], v_send.at[k], v_recv.at[k],
            device_id=(lat, partner(k)), device_id_type=MESH)

    def in_copy(d):
        return pltpu.make_async_remote_copy(
            inw, in_full.at[pl.ds(pl.multiple_of(lat * 32, 32), 32)], i_send.at[d], i_recv.at[d],
            device_id=((lat + d) % BANDS, lon), device_id_type=MESH)

    def mix_copy(d):
        return pltpu.make_async_remote_copy(
            mixw, mix_out.at[pl.ds(pl.multiple_of(lat * 64, 64), 64)], m_send.at[d], m_recv.at[d],
            device_id=((lat + d) % BANDS, lon), device_id_type=MESH)

    for k in range(1, TILES):
        cell_copy(k).start()
    for d in range(1, BANDS):
        in_copy(d).start()
    for d in range(1, BANDS):
        mix_copy(d).start()
    own_in = pltpu.make_async_copy(inw, in_full.at[pl.ds(pl.multiple_of(lat * 32, 32), 32)], l_sem.at[0])
    own_mix = pltpu.make_async_copy(mixw, mix_out.at[pl.ds(pl.multiple_of(lat * 64, 64), 64)], l_sem.at[1])
    own_in.start()
    own_mix.start()

    for g in range(GROUPS):
        picks = []
        for j in range(GROUP):
            chosen = wide((tid == partner(GROUP * g + j)).astype(F32))
            picks.append(jnp.concatenate([onehot[16 * i : 16 * i + 16] * chosen for i in range(CAP // 16)], axis=0))
        picked = jnp.dot(jnp.concatenate(picks, axis=0), vals[...], preferred_element_type=F32).astype(BF16)
        for j in range(GROUP):
            k = GROUP * g + j
            if k == 0:
                recv[0] = picked[:CAP]
            else:
                sbuf[k] = picked[CAP * j : CAP * j + CAP]
                value_copy(k).start()

    for k in range(1, TILES):
        cell_copy(k).wait_recv()
    counts[...] = jnp.zeros_like(counts)
    place = iota((SIDE, KDIM), 0).astype(F32)
    for g in range(GROUPS):
        hits = []
        for line, near, gain, room, e_f in (
            (0, near_r, gain_r, room_r, er_f),
            (1, near_c, gain_c, room_c, ec_f),
        ):
            spot = jnp.concatenate([crecv[GROUP * g + j][line : line + 1] for j in range(GROUP)], axis=1)
            spot = jnp.where(spot == 0.0, -100.0, spot - 1.0)
            gap = place - spot
            square = gap * gap
            weight = jnp.exp(square * (-1.0 / 36.0))
            near[g] = square.astype(BF16)
            gain[g] = weight.astype(BF16)
            room[g] = 36.0 - square
            e_f[g] = weight
            hits.append((square == 0.0).astype(F32).astype(BF16))
        counts[...] += nt_dot(hits[1], hits[0])

    gap = jnp.abs(iota((SIDE, SIDE), 0) - iota((SIDE, SIDE), 1))
    fall = jnp.exp((gap * gap).astype(F32) * (-1.0 / 36.0))
    density = jnp.zeros((SIDE, SIDE), F32)
    for half, least, most in RINGS:
        across = exact_dot(jnp.where(gap <= half, fall, 0.0), counts[...])
        density = density + exact_dot(across, jnp.where((gap >= least) & (gap <= most), fall, 0.0))
    lane = iota((SIDE, SIDE), 1)

    def spread(r, _):
        column = jnp.sum(jnp.where(lane == r, density, 0.0), axis=1, keepdims=True)
        recip[pl.ds(pl.multiple_of(r * SIDE, SIDE), SIDE), :] = jnp.broadcast_to(1.0 / (column + 1.0), (SIDE, 128))
        return 0

    lax.fori_loop(0, SIDE, spread, 0)

    def weigh(room, e_f, near, gain, g, r):
        rest = wide(room[g, pl.ds(r, 1), :])
        scale = wide(e_f[g, pl.ds(r, 1), :])
        return [
            jnp.where(near[g, 16 * i : 16 * i + 16, :] <= rest, gain[g, 16 * i : 16 * i + 16, :], jnp.zeros((), BF16)) * scale
            for i in range(SIDE // 16)
        ]

    def group_values(g):
        return recv[pl.ds(GROUP * g, GROUP)].reshape(KDIM, NCH)

    def edges(g):
        pieces = (
            weigh(room_r, er_f, near_c, gain_c, g, 0)
            + weigh(room_r, er_f, near_c, gain_c, g, SIDE - 1)
            + weigh(room_c, ec_f, near_r, gain_r, g, 0)
            + weigh(room_c, ec_f, near_r, gain_r, g, SIDE - 1)
        )
        webuf[...] = jnp.concatenate(pieces, axis=0)
        return jnp.dot(webuf[...], group_values(g), preferred_element_type=F32)

    def block(g, n):
        for rr in range(BLOCK_ROWS):
            pieces = weigh(room_r, er_f, near_c, gain_c, g, n * BLOCK_ROWS + rr)
            wbuf[SIDE * rr : SIDE * rr + SIDE] = jnp.concatenate(pieces, axis=0)
        return jnp.dot(wbuf[...], group_values(g), preferred_element_type=F32)

    for g in range(GROUPS - 1):
        for j in range(GROUP):
            if GROUP * g + j:
                value_copy(GROUP * g + j).wait_recv()
        if g == 0:
            eacc[...] = edges(g)
        else:
            eacc[...] += edges(g)

        def step(n, _, g=g):
            span = pl.ds(pl.multiple_of(n * BLOCK, BLOCK), BLOCK)
            if g == 0:
                acc[span, :] = block(g, n)
            else:
                acc[span, :] += block(g, n)
            return 0

        lax.fori_loop(0, BLOCKS, step, 0)

    last = GROUPS - 1
    own_in.wait()
    for d in range(1, BANDS):
        in_copy(d).wait_recv()
    for j in range(GROUP):
        value_copy(GROUP * last + j).wait_recv()

    inverse = jnp.concatenate(
        [
            recip[0:SIDE, :],
            recip[CELLS - SIDE : CELLS, :],
            recip[pl.ds(0, SIDE, stride=SIDE), :],
            recip[pl.ds(SIDE - 1, SIDE, stride=SIDE), :],
        ],
        axis=0,
    )
    observed = ((eacc[...] + edges(last)) * jnp.concatenate([inverse, inverse], axis=1)).astype(BF16)
    feats = jnp.dot(observed, in_full[...], preferred_element_type=F32)
    ebuf[...] = feats.astype(BF16).reshape(4, SIDE, LATENT)
    for n, at in enumerate((0, SIDE - 1, SIDE, 2 * SIDE - 1)):
        cbuf[n] = jnp.broadcast_to(feats[at : at + 1], (16, LATENT)).astype(BF16)

    def edge_copy(n):
        target = ((north, lon), (south, lon), (lat, west), (lat, east))[n]
        landing = (down, up, right, left)[n]
        return pltpu.make_async_remote_copy(
            ebuf.at[n], landing, e_send.at[n], e_recv.at[n], device_id=target, device_id_type=MESH)

    def corner_copy(n):
        target = ((north, west), (north, east), (south, west), (south, east))[n]
        return pltpu.make_async_remote_copy(
            cbuf.at[n], corners.at[3 - n], k_send.at[n], k_recv.at[n], device_id=target, device_id_type=MESH)

    for n in range(4):
        edge_copy(n).start()
    for n in range(4):
        corner_copy(n).start()

    def h_copy(n):
        span = pl.ds(pl.multiple_of(n * BLOCK, BLOCK), BLOCK)
        return pltpu.make_async_copy(hbuf.at[span], h_out.at[span], h_sem.at[n])

    def finish(n, _):
        span = pl.ds(pl.multiple_of(n * BLOCK, BLOCK), BLOCK)
        inverse = recip[span, :]
        total = acc[span, :] + block(last, n)
        observed = (total * jnp.concatenate([inverse, inverse], axis=1)).astype(BF16)
        hbuf[span, :] = jnp.dot(observed, in_full[...], preferred_element_type=F32).astype(BF16)
        h_copy(n).start()
        return 0

    lax.fori_loop(0, BLOCKS, finish, 0)

    for n in range(BLOCKS):
        h_copy(n).wait()
    own_mix.wait()
    for k in range(1, TILES):
        cell_copy(k).wait_send()
        value_copy(k).wait_send()
    for d in range(1, BANDS):
        in_copy(d).wait_send()
        mix_copy(d).wait_send()
        mix_copy(d).wait_recv()
    for n in range(4):
        edge_copy(n).wait_send()
        edge_copy(n).wait_recv()
        corner_copy(n).wait_send()
        corner_copy(n).wait_recv()


def encode(vals, tile, cell, inw, mixw):
    vmem = pl.BlockSpec(memory_space=pltpu.VMEM)
    hbm = pl.BlockSpec(memory_space=pl.ANY)
    dma = pltpu.SemaphoreType.DMA
    edge = jax.ShapeDtypeStruct((SIDE, LATENT), BF16)
    return pl.pallas_call(
        encode_kernel,
        out_shape=[
            jax.ShapeDtypeStruct((CELLS, LATENT), BF16),
            edge, edge, edge, edge,
            jax.ShapeDtypeStruct((4, 16, LATENT), BF16),
            jax.ShapeDtypeStruct((LATENT, LATENT), BF16),
        ],
        in_specs=[vmem] * 5,
        out_specs=[hbm] * 7,
        scratch_shapes=[
            pltpu.VMEM((CAP, OWN), BF16),
            pltpu.VMEM((TILES, 8, CAP), F32),
            pltpu.VMEM((TILES, 8, CAP), F32),
            pltpu.VMEM((TILES, CAP, NCH), BF16),
            pltpu.VMEM((TILES, CAP, NCH), BF16),
            pltpu.VMEM((NCH, LATENT), BF16),
        ]
        + [pltpu.VMEM((GROUPS, SIDE, KDIM), BF16)] * 4
        + [pltpu.VMEM((GROUPS, SIDE, KDIM), F32)] * 4
        + [
            pltpu.VMEM((SIDE, SIDE), F32),
            pltpu.VMEM((CELLS, 128), F32),
            pltpu.VMEM((BLOCK, KDIM), BF16),
            pltpu.VMEM((CELLS, NCH), F32),
            pltpu.VMEM((4 * SIDE, NCH), F32),
            pltpu.VMEM((4 * SIDE, KDIM), BF16),
            pltpu.VMEM((4, SIDE, LATENT), BF16),
            pltpu.VMEM((4, 16, LATENT), BF16),
            pltpu.VMEM((CELLS, LATENT), BF16),
        ]
        + [dma((TILES,))] * 4
        + [dma((BANDS,))] * 4
        + [dma((4,))] * 4
        + [dma((BLOCKS,)), dma((2,))],
        compiler_params=pltpu.CompilerParams(
            collective_id=0, has_side_effects=True, vmem_limit_bytes=48 * 1024 * 1024
        ),
        name="encode",
    )(vals, tile, cell, inw, mixw)


ROWS = 4
STEPS = SIDE // ROWS
LOADS = 8
EDGE = 8


def mix_kernel(h, up, down, left, right, corners, kern, gain, mix, out, hb, hf, nb, ss, h_sem):
    i = pl.program_id(0)
    lat = lax.axis_index("lat")
    size = SIDE // LOADS

    def load(n):
        span = pl.ds(pl.multiple_of(n * size, size), size)
        return pltpu.make_async_copy(h.at[span], hb.at[span], h_sem.at[n])

    def widen(n):
        load(n).wait()
        for rr in range(size):
            r = n * size + rr
            hf[r + 1, EDGE : EDGE + SIDE, :] = hb[r].astype(F32)

    @pl.when(i == 0)
    def _():
        for n in range(LOADS):
            load(n).start()
        above = jnp.where(lat > 0, 1.0, 0.0)
        below = jnp.where(lat < BANDS - 1, 1.0, 0.0)
        hf[0, EDGE : EDGE + SIDE, :] = up[...].astype(F32) * above
        hf[SIDE + 1, EDGE : EDGE + SIDE, :] = down[...].astype(F32) * below
        for n, (r, c, keep) in enumerate(
            (
                (0, EDGE - 1, above),
                (0, EDGE + SIDE, above),
                (SIDE + 1, EDGE - 1, below),
                (SIDE + 1, EDGE + SIDE, below),
            )
        ):
            hf[r, c : c + 1, :] = corners[n].astype(F32)[0:1] * keep
        lf = left[...].astype(F32)
        rt = right[...].astype(F32)
        for r in range(SIDE):
            hf[r + 1, EDGE - 1 : EDGE, :] = lf[r : r + 1]
            hf[r + 1, EDGE + SIDE : EDGE + SIDE + 1, :] = rt[r : r + 1]
        widen(0)

    @pl.when((i % 2 == 0) & (i // 2 + 1 < LOADS))
    def _():
        widen(i // 2 + 1)

    r0 = i * ROWS
    for l in range(LATENT // 128):
        lanes = slice(128 * l, 128 * l + 128)
        taps = [jnp.broadcast_to(kern[t : t + 1, lanes], (8, 128)) for t in range(9)]
        for cb in range(SIDE // 8):
            sums = [None] * ROWS
            for rr in range(ROWS + 2):
                for b in range(3):
                    start = EDGE + 8 * cb + b - 1
                    seen = hf[r0 + rr, start : start + 8, lanes]
                    for a in range(3):
                        o = rr - a
                        if 0 <= o < ROWS:
                            term = seen * taps[3 * a + b]
                            sums[o] = term if sums[o] is None else sums[o] + term
            for o in range(ROWS):
                at = slice(SIDE * o + 8 * cb, SIDE * o + 8 * cb + 8)
                nb[at, lanes] = sums[o]
                if l == 0:
                    ss[at, :] = sums[o] * sums[o]
                else:
                    ss[at, :] += sums[o] * sums[o]
    mean = jnp.sum(ss[...], axis=1, keepdims=True) * (1.0 / LATENT)
    normed = (nb[...] * lax.rsqrt(mean + 1e-6) * gain[...]).astype(BF16)
    half = jnp.dot(normed, mix[...], preferred_element_type=F32) * 0.5
    base = hf[pl.ds(r0 + 1, ROWS), EDGE : EDGE + SIDE, :].reshape(ROWS * SIDE, LATENT)
    out[...] = (base + (half + half * jnp.tanh(half))).astype(BF16).reshape(ROWS, SIDE, LATENT)


def mix_layer(h, up, down, left, right, corners, kern, gain, mix):
    vmem = pl.BlockSpec(memory_space=pltpu.VMEM)
    return pl.pallas_call(
        mix_kernel,
        out_shape=jax.ShapeDtypeStruct((SIDE, SIDE, LATENT), BF16),
        grid=(STEPS,),
        in_specs=[pl.BlockSpec(memory_space=pl.ANY)] + [vmem] * 8,
        out_specs=pl.BlockSpec((ROWS, SIDE, LATENT), lambda i: (i, 0, 0)),
        scratch_shapes=[
            pltpu.VMEM((SIDE, SIDE, LATENT), BF16),
            pltpu.VMEM((SIDE + 2, SIDE + 2 * EDGE, LATENT), F32),
            pltpu.VMEM((ROWS * SIDE, LATENT), F32),
            pltpu.VMEM((ROWS * SIDE, 128), F32),
            pltpu.SemaphoreType.DMA((LOADS,)),
        ],
        compiler_params=pltpu.CompilerParams(vmem_limit_bytes=48 * 1024 * 1024),
        name="mix_layer",
    )(h, up, down, left, right, corners, kern, gain, mix)


def local(reading_values, reading_tile, reading_cell, in_weight, kernel, norm_gain, mix_weight):
    h, up, down, left, right, corners, mix = encode(
        reading_values,
        reading_tile.reshape(1, OWN),
        reading_cell.reshape(1, OWN),
        in_weight,
        mix_weight,
    )
    return mix_layer(
        h.reshape(SIDE, SIDE, LATENT), up, down, left, right, corners, kernel, norm_gain.reshape(1, LATENT), mix
    )


def solution(mesh):
    placed = (
        P(("lat", "lon"), None),
        P(("lat", "lon"), None),
        P(("lat", "lon")),
        P("lat", None),
        P(),
        P(),
        P("lat", None),
    )
    return jax.shard_map(
        local, mesh=mesh, in_specs=placed, out_specs=P("lat", "lon", None), check_vma=False
    )
```

```python
import jax
import jax.numpy as jnp
from jax import lax
from jax.experimental import pallas as pl
from jax.experimental.pallas import tpu as pltpu
from jax.sharding import PartitionSpec as P

F32 = jnp.float32
BF16 = jnp.bfloat16
MESH = pl.DeviceIdType.MESH

NCH = 256
LATENT = 512
SIDE = 64
OWN = 1024
CAP = 128
TILES = 16
BANDS = 8
GROUP = 4
GROUPS = TILES // GROUP
KDIM = GROUP * CAP
BLOCK_ROWS = 16
BLOCK = BLOCK_ROWS * SIDE
BLOCKS = SIDE // BLOCK_ROWS
CELLS = SIDE * SIDE
RINGS = ((6, 0, 0), (5, 1, 3), (4, 4, 4), (3, 5, 5), (0, 6, 6))


def iota(shape, dim):
    return lax.broadcasted_iota(jnp.int32, shape, dim)


def nt_dot(a, b):
    return lax.dot_general(a, b, (((1,), (1,)), ((), ())), preferred_element_type=F32)


def exact_dot(a, b):
    return jnp.dot(a, b, preferred_element_type=F32, precision=lax.Precision.HIGHEST)


def wide(row):
    return jnp.broadcast_to(row, (16, row.shape[1])).astype(BF16)


def encode_kernel(
    vals_in, tile_in, cell_in, inw, mixw, kern_in, gain_in,
    h_out, left, right, corners, taps, flat, mix_out,
    vals, tile, cell, kern, norm, onehot, cmsg, crecv, sbuf, recv, in_full,
    near_r, near_c, gain_r, gain_c, room_r, room_c, er_f, ec_f,
    counts, recip, wbuf, acc, eacc, webuf, ebuf, cbuf,
    v_send, v_recv, c_send, c_recv, i_send, i_recv, m_send, m_recv, e_send, e_recv, k_send, k_recv,
    l_sem,
):
    lat = lax.axis_index("lat")
    lon = lax.axis_index("lon")
    east, west = (lon + 1) % TILES, (lon + TILES - 1) % TILES
    north, south = (lat + BANDS - 1) % BANDS, (lat + 1) % BANDS
    lon_x, lon_y = lon // 4, lon % 4

    def partner(k):
        return ((lon_x + k // 4) % 4) * 4 + (lon_y + k % 4) % 4

    own_copies = []
    for n, (source, landing) in enumerate(
        (
            (tile_in, tile),
            (cell_in, cell),
            (vals_in, vals),
            (kern_in, kern),
            (gain_in, norm),
            (inw, in_full.at[pl.ds(pl.multiple_of(lat * 32, 32), 32)]),
            (mixw, mix_out.at[pl.ds(pl.multiple_of(lat * 64, 64), 64)]),
        )
    ):
        own_copies.append(pltpu.make_async_copy(source, landing, l_sem.at[n]))
        own_copies[n].start()

    barrier = pltpu.get_barrier_semaphore()

    def greet(where):
        pl.semaphore_signal(barrier, inc=1, device_id=where, device_id_type=MESH)

    for k in range(1, TILES):
        greet((lat, partner(k)))
    for d in range(1, BANDS):
        greet(((lat + d) % BANDS, lon))
    for a in (north, south):
        for b in (west, east):
            greet((a, b))

    own_copies[0].wait()
    tid = tile[...]
    belongs = (iota((TILES, OWN), 0) == tid).astype(F32)
    before = (iota((128, 128), 0) < iota((128, 128), 1)).astype(F32).astype(BF16)
    carry = jnp.zeros((TILES, 1), F32)
    ranks = []
    for b in range(OWN // 128):
        part = belongs[:, 128 * b : 128 * b + 128]
        within = jnp.dot(part.astype(BF16), before, preferred_element_type=F32)
        ranks.append(jnp.sum(part * (within + carry), axis=0, keepdims=True))
        carry = carry + jnp.sum(part, axis=1, keepdims=True)
    rank = jnp.concatenate(ranks, axis=1)
    onehot[...] = (iota((CAP, OWN), 0).astype(F32) == rank).astype(F32).astype(BF16)

    own_copies[1].wait()
    rows = (cell[...] >> 6).astype(F32) + 1.0
    cols = (cell[...] & 63).astype(F32) + 1.0
    line = iota((8 * TILES, OWN), 0)
    which = line & 7
    info = jnp.where(which == 0, rows, jnp.where(which == 1, cols, 0.0))
    info = jnp.where((line >> 3) == tid, info, 0.0).astype(BF16)
    cmsg[...] = nt_dot(info, onehot[...]).reshape(TILES, 8, CAP)
    crecv[0] = cmsg[lon]

    pl.semaphore_wait(barrier, TILES - 1 + BANDS - 1 + 4)

    def cell_copy(k):
        return pltpu.make_async_remote_copy(
            cmsg.at[partner(k)], crecv.at[k], c_send.at[k], c_recv.at[k],
            device_id=(lat, partner(k)), device_id_type=MESH)

    def value_copy(k):
        return pltpu.make_async_remote_copy(
            sbuf.at[k], recv.at[k], v_send.at[k], v_recv.at[k],
            device_id=(lat, partner(k)), device_id_type=MESH)

    def in_copy(d):
        return pltpu.make_async_remote_copy(
            inw, in_full.at[pl.ds(pl.multiple_of(lat * 32, 32), 32)], i_send.at[d], i_recv.at[d],
            device_id=((lat + d) % BANDS, lon), device_id_type=MESH)

    def mix_copy(d):
        return pltpu.make_async_remote_copy(
            mixw, mix_out.at[pl.ds(pl.multiple_of(lat * 64, 64), 64)], m_send.at[d], m_recv.at[d],
            device_id=((lat + d) % BANDS, lon), device_id_type=MESH)

    for k in range(1, TILES):
        cell_copy(k).start()
    for d in range(1, BANDS):
        in_copy(d).start()
    for d in range(1, BANDS):
        mix_copy(d).start()
    own_copies[2].wait()

    for g in range(GROUPS):
        picks = []
        for j in range(GROUP):
            chosen = wide((tid == partner(GROUP * g + j)).astype(F32))
            picks.append(jnp.concatenate([onehot[16 * i : 16 * i + 16] * chosen for i in range(CAP // 16)], axis=0))
        picked = jnp.dot(jnp.concatenate(picks, axis=0), vals[...], preferred_element_type=F32).astype(BF16)
        for j in range(GROUP):
            k = GROUP * g + j
            if k == 0:
                recv[0] = picked[:CAP]
            else:
                sbuf[k] = picked[CAP * j : CAP * j + CAP]
                value_copy(k).start()

    for k in range(1, TILES):
        cell_copy(k).wait_recv()
    counts[...] = jnp.zeros_like(counts)
    place = iota((SIDE, KDIM), 0).astype(F32)
    for g in range(GROUPS):
        hits = []
        for line, near, gain, room, e_f in (
            (0, near_r, gain_r, room_r, er_f),
            (1, near_c, gain_c, room_c, ec_f),
        ):
            spot = jnp.concatenate([crecv[GROUP * g + j][line : line + 1] for j in range(GROUP)], axis=1)
            spot = jnp.where(spot == 0.0, -100.0, spot - 1.0)
            gap = place - spot
            square = gap * gap
            weight = jnp.exp(square * (-1.0 / 36.0))
            near[g] = square.astype(BF16)
            gain[g] = weight.astype(BF16)
            room[g] = 36.0 - square
            e_f[g] = weight
            hits.append((square == 0.0).astype(F32).astype(BF16))
        counts[...] += nt_dot(hits[1], hits[0])

    gap = jnp.abs(iota((SIDE, SIDE), 0) - iota((SIDE, SIDE), 1))
    fall = jnp.exp((gap * gap).astype(F32) * (-1.0 / 36.0))
    density = jnp.zeros((SIDE, SIDE), F32)
    for half, least, most in RINGS:
        across = exact_dot(jnp.where(gap <= half, fall, 0.0), counts[...])
        density = density + exact_dot(across, jnp.where((gap >= least) & (gap <= most), fall, 0.0))
    inverse = 1.0 / (density + 1.0)
    for r in range(SIDE):
        recip[SIDE * r : SIDE * r + SIDE, :] = jnp.broadcast_to(inverse[:, r : r + 1], (SIDE, 128))

    own_copies[3].wait()
    own_copies[4].wait()
    taps[...] = kern[...] * norm[...]
    square = 1.0 / (norm[...] * norm[...])
    for n in range(LATENT // 128):
        part = jnp.broadcast_to(square[:, 128 * n : 128 * n + 128], (128, 128))
        flat[128 * n : 128 * n + 128, :] = part.T.astype(BF16)

    def weigh(room, e_f, near, gain, g, r):
        rest = wide(room[g, pl.ds(r, 1), :])
        scale = wide(e_f[g, pl.ds(r, 1), :])
        return [
            jnp.where(near[g, 16 * i : 16 * i + 16, :] <= rest, gain[g, 16 * i : 16 * i + 16, :], jnp.zeros((), BF16)) * scale
            for i in range(SIDE // 16)
        ]

    def group_values(g):
        return recv[pl.ds(GROUP * g, GROUP)].reshape(KDIM, NCH)

    def edges(g):
        pieces = (
            weigh(room_r, er_f, near_c, gain_c, g, 0)
            + weigh(room_r, er_f, near_c, gain_c, g, SIDE - 1)
            + weigh(room_c, ec_f, near_r, gain_r, g, 0)
            + weigh(room_c, ec_f, near_r, gain_r, g, SIDE - 1)
        )
        webuf[...] = jnp.concatenate(pieces, axis=0)
        return jnp.dot(webuf[...], group_values(g), preferred_element_type=F32)

    def prepare(g, n):
        for rr in range(BLOCK_ROWS):
            pieces = weigh(room_r, er_f, near_c, gain_c, g, n * BLOCK_ROWS + rr)
            wbuf[n % 2, SIDE * rr : SIDE * rr + SIDE] = jnp.concatenate(pieces, axis=0)

    def product(g, n):
        return jnp.dot(wbuf[n % 2], group_values(g), preferred_element_type=F32)

    for g in range(GROUPS - 1):
        for j in range(GROUP):
            if GROUP * g + j:
                value_copy(GROUP * g + j).wait_recv()
        if g == 0:
            eacc[...] = edges(g)
        else:
            eacc[...] += edges(g)

        prepare(g, 0)
        for n in range(BLOCKS):
            span = slice(n * BLOCK, n * BLOCK + BLOCK)
            if n + 1 < BLOCKS:
                prepare(g, n + 1)
            if g == 0:
                acc[span, :] = product(g, n)
            else:
                acc[span, :] += product(g, n)

    last = GROUPS - 1
    own_copies[5].wait()
    for d in range(1, BANDS):
        in_copy(d).wait_recv()
    for j in range(GROUP):
        value_copy(GROUP * last + j).wait_recv()

    inverse = jnp.concatenate(
        [
            recip[0:SIDE, :],
            recip[CELLS - SIDE : CELLS, :],
            recip[pl.ds(0, SIDE, stride=SIDE), :],
            recip[pl.ds(SIDE - 1, SIDE, stride=SIDE), :],
        ],
        axis=0,
    )
    observed = ((eacc[...] + edges(last)) * jnp.concatenate([inverse, inverse], axis=1)).astype(BF16)
    feats = jnp.dot(observed, in_full[...], preferred_element_type=F32)
    ebuf[...] = feats.astype(BF16).reshape(4, SIDE, LATENT)
    for n, at in enumerate((0, SIDE - 1, SIDE, 2 * SIDE - 1)):
        cbuf[n] = jnp.broadcast_to(feats[at : at + 1], (16, LATENT)).astype(BF16)

    def edge_copy(n):
        target = ((north, lon), (south, lon), (lat, west), (lat, east))[n]
        landing = (h_out.at[pl.ds(CELLS + SIDE, SIDE)], h_out.at[pl.ds(0, SIDE)], right, left)[n]
        return pltpu.make_async_remote_copy(
            ebuf.at[n], landing, e_send.at[n], e_recv.at[n], device_id=target, device_id_type=MESH)

    def corner_copy(n):
        target = ((north, west), (north, east), (south, west), (south, east))[n]
        return pltpu.make_async_remote_copy(
            cbuf.at[n], corners.at[3 - n], k_send.at[n], k_recv.at[n], device_id=target, device_id_type=MESH)

    for n in range(4):
        edge_copy(n).start()
    for n in range(4):
        corner_copy(n).start()

    prepare(last, 0)
    for n in range(BLOCKS):
        span = slice(n * BLOCK, n * BLOCK + BLOCK)
        if n + 1 < BLOCKS:
            prepare(last, n + 1)
        inverse = recip[span, :]
        total = acc[span, :] + product(last, n)
        observed = (total * jnp.concatenate([inverse, inverse], axis=1)).astype(BF16)
        h_out[SIDE + n * BLOCK : SIDE + n * BLOCK + BLOCK, :] = jnp.dot(
            observed, in_full[...], preferred_element_type=F32
        ).astype(BF16)

    own_copies[6].wait()
    for k in range(1, TILES):
        cell_copy(k).wait_send()
        value_copy(k).wait_send()
    for d in range(1, BANDS):
        in_copy(d).wait_send()
        mix_copy(d).wait_send()
        mix_copy(d).wait_recv()
    for n in range(4):
        edge_copy(n).wait_send()
        edge_copy(n).wait_recv()
        corner_copy(n).wait_send()
        corner_copy(n).wait_recv()


def encode(vals, tile, cell, inw, mixw, kern, gain):
    vmem = pl.BlockSpec(memory_space=pltpu.VMEM)
    hbm = pl.BlockSpec(memory_space=pltpu.HBM)
    dma = pltpu.SemaphoreType.DMA
    edge = jax.ShapeDtypeStruct((SIDE, LATENT), BF16)
    return pl.pallas_call(
        encode_kernel,
        out_shape=[
            jax.ShapeDtypeStruct((CELLS + 2 * SIDE, LATENT), BF16),
            edge,
            edge,
            jax.ShapeDtypeStruct((4, 16, LATENT), BF16),
            jax.ShapeDtypeStruct((9, LATENT), F32),
            jax.ShapeDtypeStruct((LATENT, 128), BF16),
            jax.ShapeDtypeStruct((LATENT, LATENT), BF16),
        ],
        in_specs=[hbm] * 7,
        out_specs=[vmem] * 7,
        scratch_shapes=[
            pltpu.VMEM((OWN, NCH), BF16),
            pltpu.VMEM((1, OWN), jnp.int32),
            pltpu.VMEM((1, OWN), jnp.int32),
            pltpu.VMEM((9, LATENT), F32),
            pltpu.VMEM((1, LATENT), F32),
            pltpu.VMEM((CAP, OWN), BF16),
            pltpu.VMEM((TILES, 8, CAP), F32),
            pltpu.VMEM((TILES, 8, CAP), F32),
            pltpu.VMEM((TILES, CAP, NCH), BF16),
            pltpu.VMEM((TILES, CAP, NCH), BF16),
            pltpu.VMEM((NCH, LATENT), BF16),
        ]
        + [pltpu.VMEM((GROUPS, SIDE, KDIM), BF16)] * 4
        + [pltpu.VMEM((GROUPS, SIDE, KDIM), F32)] * 4
        + [
            pltpu.VMEM((SIDE, SIDE), F32),
            pltpu.VMEM((CELLS, 128), F32),
            pltpu.VMEM((2, BLOCK, KDIM), BF16),
            pltpu.VMEM((CELLS, NCH), F32),
            pltpu.VMEM((4 * SIDE, NCH), F32),
            pltpu.VMEM((4 * SIDE, KDIM), BF16),
            pltpu.VMEM((4, SIDE, LATENT), BF16),
            pltpu.VMEM((4, 16, LATENT), BF16),
        ]
        + [dma((TILES,))] * 4
        + [dma((BANDS,))] * 4
        + [dma((4,))] * 4
        + [dma((7,))],
        compiler_params=pltpu.CompilerParams(
            collective_id=0, has_side_effects=True, vmem_limit_bytes=32 * 1024 * 1024
        ),
        name="encode",
    )(vals, tile, cell, inw, mixw, kern, gain)


ROWS = 8
PART = 4
STEPS = SIDE // ROWS
EDGE = 8
CHUNKS = LATENT // 128


def mix_kernel(h, left, right, corners, taps, flat, mix, out, hf, nb, sq):
    i = pl.program_id(0)
    lat = lax.axis_index("lat")
    nil = i // STEPS

    def widen(p):
        for l in range(CHUNKS):
            rows = h[pl.ds(pl.multiple_of(p * SIDE, SIDE), SIDE), 128 * l : 128 * l + 128]
            hf[l, p, EDGE : EDGE + SIDE, :] = rows.astype(F32)

    @pl.when(i == 0)
    def _():
        for p in range(ROWS + 2):
            widen(p)
        lf = left[...].astype(F32)
        rt = right[...].astype(F32)
        for l in range(CHUNKS):
            lanes = slice(128 * l, 128 * l + 128)
            for r in range(SIDE):
                hf[l, r + 1, EDGE - 1 : EDGE, :] = lf[r : r + 1, lanes]
                hf[l, r + 1, EDGE + SIDE : EDGE + SIDE + 1, :] = rt[r : r + 1, lanes]
            for n, (r, c) in enumerate(((0, EDGE - 1), (0, EDGE + SIDE), (SIDE + 1, EDGE - 1), (SIDE + 1, EDGE + SIDE))):
                hf[l, r, c : c + 1, :] = corners[n].astype(F32)[0:1, lanes]

    @pl.when((i == 0) & (lat == 0))
    def _():
        for l in range(CHUNKS):
            hf[l, 0] = jnp.zeros((SIDE + 2 * EDGE, 128), F32)

    @pl.when((i == STEPS - 1) & (lat == BANDS - 1))
    def _():
        for l in range(CHUNKS):
            hf[l, SIDE + 1] = jnp.zeros((SIDE + 2 * EDGE, 128), F32)

    r0 = i * ROWS

    def gather(part):
        for l in range(CHUNKS):
            lanes = slice(128 * l, 128 * l + 128)
            tap = [jnp.broadcast_to(taps[t : t + 1, lanes], (8, 128)) for t in range(9)]
            for cb in range(SIDE // 16):
                halves = []
                for u in range(2):
                    sums = [None] * PART
                    for rr in range(PART + 2):
                        for b in range(3):
                            start = nil + EDGE + 16 * cb + 8 * u + b - 1
                            if b == 1:
                                start = EDGE + 16 * cb + 8 * u
                            seen = hf[l, r0 + PART * part + rr, pl.ds(start, 8), :]
                            for a in range(3):
                                o = rr - a
                                if 0 <= o < PART:
                                    term = seen * tap[3 * a + b]
                                    sums[o] = term if sums[o] is None else sums[o] + term
                    halves.append(sums)
                for o in range(PART):
                    pair = jnp.concatenate([halves[0][o], halves[1][o]], axis=0)
                    at = slice(SIDE * o + 16 * cb, SIDE * o + 16 * cb + 16)
                    nb[part, at, lanes] = pair.astype(BF16)
                    sq[part, at, lanes] = (pair * pair).astype(BF16)

    def finish(part):
        mean = jnp.dot(sq[part], flat[...], preferred_element_type=F32) * (1.0 / LATENT)
        scale = lax.rsqrt(mean + 1e-6) * 0.5
        for q in range(2):
            mixed = jnp.dot(nb[part], mix[:, 256 * q : 256 * q + 256], preferred_element_type=F32)
            for m in range(2):
                l = 2 * q + m
                half = mixed[:, 128 * m : 128 * m + 128] * scale
                base = hf[l, pl.ds(r0 + PART * part + 1, PART), EDGE : EDGE + SIDE, :].reshape(PART * SIDE, 128)
                done = base + (half + half * jnp.tanh(half))
                out[PART * part : PART * part + PART, :, 128 * l : 128 * l + 128] = done.astype(BF16).reshape(PART, SIDE, 128)

    parts = ROWS // PART
    for part in range(parts):
        gather(part)
        if part:
            finish(part - 1)
    finish(parts - 1)

    @pl.when(i < STEPS - 1)
    def _():
        for rr in range(ROWS):
            widen(r0 + ROWS + 2 + rr)


def mix_layer(h, left, right, corners, taps, flat, mix):
    vmem = pl.BlockSpec(memory_space=pltpu.VMEM)
    return pl.pallas_call(
        mix_kernel,
        out_shape=jax.ShapeDtypeStruct((SIDE, SIDE, LATENT), BF16),
        grid=(STEPS,),
        in_specs=[vmem] * 7,
        out_specs=pl.BlockSpec((ROWS, SIDE, LATENT), lambda i: (i, 0, 0)),
        scratch_shapes=[
            pltpu.VMEM((CHUNKS, SIDE + 2, SIDE + 2 * EDGE, 128), F32),
            pltpu.VMEM((ROWS // PART, PART * SIDE, LATENT), BF16),
            pltpu.VMEM((ROWS // PART, PART * SIDE, LATENT), BF16),
        ],
        compiler_params=pltpu.CompilerParams(vmem_limit_bytes=32 * 1024 * 1024),
        name="mix_layer",
    )(h, left, right, corners, taps, flat, mix)


def local(reading_values, reading_tile, reading_cell, in_weight, kernel, norm_gain, mix_weight):
    operands = (
        reading_values,
        reading_tile.reshape(1, OWN),
        reading_cell.reshape(1, OWN),
        in_weight,
        mix_weight,
        kernel,
        norm_gain.reshape(1, LATENT),
    )
    return mix_layer(*encode(*(pltpu.with_memory_space_constraint(x, pltpu.HBM) for x in operands)))


def solution(mesh):
    placed = (
        P(("lat", "lon"), None),
        P(("lat", "lon"), None),
        P(("lat", "lon")),
        P("lat", None),
        P(),
        P(),
        P("lat", None),
    )
    return jax.shard_map(
        local, mesh=mesh, in_specs=placed, out_specs=P("lat", "lon", None), check_vma=False
    )
```

```python
import functools

import jax
import jax.numpy as jnp
from jax import lax
from jax.experimental import pallas as pl
from jax.experimental.pallas import tpu as pltpu
from jax.sharding import PartitionSpec as P

F32 = jnp.float32
BF16 = jnp.bfloat16
MESH = pl.DeviceIdType.MESH

NCH = 256
LATENT = 512
SIDE = 64
OWN = 1024
CAP = 128
TILES = 16
BANDS = 8
GROUP = 4
GROUPS = TILES // GROUP
KDIM = GROUP * CAP
SLOTS = TILES * CAP
PASSES = ((0, 4), (4, 8), (8, 12), (12, 14), (14, 16))
LAST = (PASSES[-1][1] - PASSES[-1][0]) * CAP
STEPS = ((0, 0), (2, 2), (2, 1), (1, 2), (2, 3), (3, 2), (2, 0), (0, 2), (1, 1), (3, 3), (1, 3), (3, 1), (1, 0), (0, 1), (3, 0), (0, 3))
BLOCK_ROWS = 16
BLOCK = BLOCK_ROWS * SIDE
BLOCKS = SIDE // BLOCK_ROWS
CELLS = SIDE * SIDE
RINGS = ((6, 0, 0), (5, 1, 3), (4, 4, 4), (3, 5, 5), (0, 6, 6))


def iota(shape, dim):
    return lax.broadcasted_iota(jnp.int32, shape, dim)


def nt_dot(a, b):
    return lax.dot_general(a, b, (((1,), (1,)), ((), ())), preferred_element_type=F32)


def exact_dot(a, b):
    return jnp.dot(a, b, preferred_element_type=F32, precision=lax.Precision.HIGHEST)


def wide(row):
    return jnp.broadcast_to(row, (16, row.shape[1])).astype(BF16)


def encode_kernel(
    vals_in, tile_in, cell_in, inw, mixw, kern_in, gain_in,
    h_out, left, right, corners, taps, mix_out,
    vals, tile, cell, kern, norm, onehot, cmsg, crecv, sbuf, recv, in_full,
    near_r, near_c, gain_r, gain_c, room_r, room_c, er_f, ec_f,
    counts, recip, wbuf, wlast, acc, eacc, webuf, ebuf, cbuf,
    v_send, v_recv, c_send, c_recv, i_send, i_recv, m_send, m_recv, e_send, e_recv, k_send, k_recv,
    l_sem,
):
    lat = lax.axis_index("lat")
    lon = lax.axis_index("lon")
    always = lon < TILES
    east, west = (lon + 1) % TILES, (lon + TILES - 1) % TILES
    north, south = (lat + BANDS - 1) % BANDS, (lat + 1) % BANDS
    lon_x, lon_y = lon // 4, lon % 4

    def partner(k):
        return ((lon_x + STEPS[k][0]) % 4) * 4 + (lon_y + STEPS[k][1]) % 4

    own_copies = []
    for n, (source, landing) in enumerate(
        (
            (tile_in, tile),
            (cell_in, cell),
            (vals_in, vals),
            (kern_in, kern),
            (gain_in, norm),
            (inw, in_full.at[pl.ds(pl.multiple_of(lat * 32, 32), 32)]),
            (mixw, mix_out.at[pl.ds(pl.multiple_of(lat * 64, 64), 64)]),
        )
    ):
        own_copies.append(pltpu.make_async_copy(source, landing, l_sem.at[n]))
        own_copies[n].start()

    barrier = pltpu.get_barrier_semaphore()

    def greet(where):
        pl.semaphore_signal(barrier, inc=1, device_id=where, device_id_type=MESH)

    for k in range(1, TILES):
        greet((lat, partner(k)))
    for d in range(1, BANDS):
        greet(((lat + d) % BANDS, lon))
    for a in (north, south):
        for b in (west, east):
            greet((a, b))

    own_copies[0].wait()
    tid = tile[...]
    belongs = (iota((TILES, OWN), 0) == tid).astype(F32)
    before = (iota((128, 128), 0) < iota((128, 128), 1)).astype(F32).astype(BF16)
    carry = jnp.zeros((TILES, 1), F32)
    ranks = []
    for b in range(OWN // 128):
        part = belongs[:, 128 * b : 128 * b + 128]
        within = jnp.dot(part.astype(BF16), before, preferred_element_type=F32)
        ranks.append(jnp.sum(part * (within + carry), axis=0, keepdims=True))
        carry = carry + jnp.sum(part, axis=1, keepdims=True)
    rank = jnp.concatenate(ranks, axis=1)
    onehot[...] = (iota((CAP, OWN), 0).astype(F32) == rank).astype(F32).astype(BF16)

    own_copies[1].wait()
    rows = (cell[...] >> 6).astype(F32) + 1.0
    cols = (cell[...] & 63).astype(F32) + 1.0
    line = iota((8 * TILES, OWN), 0)
    which = line & 7
    info = jnp.where(which == 0, rows, jnp.where(which == 1, cols, 0.0))
    info = jnp.where((line >> 3) == tid, info, 0.0).astype(BF16)
    cmsg[...] = nt_dot(info, onehot[...]).reshape(TILES, 8, CAP)
    crecv[0] = cmsg[lon]

    pl.semaphore_wait(barrier, TILES - 1 + BANDS - 1 + 4)

    def cell_copy(k):
        return pltpu.make_async_remote_copy(
            cmsg.at[partner(k)], crecv.at[k], c_send.at[k], c_recv.at[k],
            device_id=(lat, partner(k)), device_id_type=MESH)

    def value_copy(k):
        return pltpu.make_async_remote_copy(
            sbuf.at[k], recv.at[k], v_send.at[k], v_recv.at[k],
            device_id=(lat, partner(k)), device_id_type=MESH)

    def in_copy(d):
        return pltpu.make_async_remote_copy(
            inw, in_full.at[pl.ds(pl.multiple_of(lat * 32, 32), 32)], i_send.at[d], i_recv.at[d],
            device_id=((lat + d) % BANDS, lon), device_id_type=MESH)

    def mix_copy(d):
        return pltpu.make_async_remote_copy(
            mixw, mix_out.at[pl.ds(pl.multiple_of(lat * 64, 64), 64)], m_send.at[d], m_recv.at[d],
            device_id=((lat + d) % BANDS, lon), device_id_type=MESH)

    own_copies[2].wait()

    def dispatch(g):
        picks = []
        for j in range(GROUP):
            chosen = wide((tid == partner(GROUP * g + j)).astype(F32))
            picks.append(jnp.concatenate([onehot[16 * i : 16 * i + 16] * chosen for i in range(CAP // 16)], axis=0))
        picked = jnp.dot(jnp.concatenate(picks, axis=0), vals[...], preferred_element_type=F32).astype(BF16)
        for j in range(GROUP):
            k = GROUP * g + j
            if k == 0:
                recv[0] = picked[:CAP]
            else:
                sbuf[k] = picked[CAP * j : CAP * j + CAP]
                value_copy(k).start()

    for g in range(GROUPS):
        pl.when(always)(functools.partial(dispatch, g))
        if g == 0:
            for k in range(1, TILES):
                cell_copy(k).start()
    for d in range(1, BANDS):
        in_copy(d).start()
    for d in range(1, BANDS):
        mix_copy(d).start()

    for k in range(1, TILES):
        cell_copy(k).wait_recv()
    counts[...] = jnp.zeros_like(counts)
    place = iota((SIDE, KDIM), 0).astype(F32)
    for g in range(GROUPS):
        hits = []
        for line, near, gain, room, e_f in (
            (0, near_r, gain_r, room_r, er_f),
            (1, near_c, gain_c, room_c, ec_f),
        ):
            spot = jnp.concatenate([crecv[GROUP * g + j][line : line + 1] for j in range(GROUP)], axis=1)
            spot = jnp.where(spot == 0.0, -100.0, spot - 1.0)
            gap = place - spot
            square = gap * gap
            weight = jnp.exp(square * (-1.0 / 36.0))
            span = slice(KDIM * g, KDIM * g + KDIM)
            near[:, span] = square.astype(BF16)
            gain[:, span] = weight.astype(BF16)
            room[:, span] = 36.0 - square
            e_f[:, span] = weight
            hits.append((square == 0.0).astype(F32).astype(BF16))
        counts[...] += nt_dot(hits[1], hits[0])

    gap = jnp.abs(iota((SIDE, SIDE), 0) - iota((SIDE, SIDE), 1))
    fall = jnp.exp((gap * gap).astype(F32) * (-1.0 / 36.0))
    density = jnp.zeros((SIDE, SIDE), F32)
    for half, least, most in RINGS:
        across = exact_dot(jnp.where(gap <= half, fall, 0.0), counts[...])
        density = density + exact_dot(across, jnp.where((gap >= least) & (gap <= most), fall, 0.0))
    inverse = 1.0 / (density + 1.0)
    for r in range(SIDE):
        recip[SIDE * r : SIDE * r + SIDE, :] = jnp.broadcast_to(inverse[:, r : r + 1], (SIDE, 128))

    own_copies[3].wait()
    own_copies[4].wait()
    taps[...] = kern[...]

    def weigh(room, e_f, near, gain, turn, r):
        span = slice(CAP * turn[0], CAP * turn[1])
        rest = wide(room[r : r + 1, span])
        scale = wide(e_f[r : r + 1, span])
        return [
            jnp.where(near[16 * i : 16 * i + 16, span] <= rest, gain[16 * i : 16 * i + 16, span], jnp.zeros((), BF16)) * scale
            for i in range(SIDE // 16)
        ]

    def turn_values(turn):
        return recv[turn[0] : turn[1]].reshape((turn[1] - turn[0]) * CAP, NCH)

    def edge_weights(turn):
        return jnp.concatenate(
            weigh(room_r, er_f, near_c, gain_c, turn, 0)
            + weigh(room_r, er_f, near_c, gain_c, turn, SIDE - 1)
            + weigh(room_c, ec_f, near_r, gain_r, turn, 0)
            + weigh(room_c, ec_f, near_r, gain_r, turn, SIDE - 1),
            axis=0,
        )

    def prepare(target, turn, n):
        width = (turn[1] - turn[0]) * CAP
        for rr in range(BLOCK_ROWS):
            pieces = weigh(room_r, er_f, near_c, gain_c, turn, n * BLOCK_ROWS + rr)
            target[SIDE * rr : SIDE * rr + SIDE, 0:width] = jnp.concatenate(pieces, axis=0)

    last = PASSES[-1]
    for p, turn in enumerate(PASSES[:-1]):
        width = (turn[1] - turn[0]) * CAP
        webuf[:, 0:width] = edge_weights(turn)
        prepare(wbuf.at[0], turn, 0)
        for k in range(*turn):
            if k:
                value_copy(k).wait_recv()
        product = jnp.dot(webuf[:, 0:width], turn_values(turn), preferred_element_type=F32)
        eacc[...] = product if p == 0 else eacc[...] + product
        for n in range(BLOCKS):
            span = slice(n * BLOCK, n * BLOCK + BLOCK)
            if n + 1 < BLOCKS:
                prepare(wbuf.at[(n + 1) % 2], turn, n + 1)
            product = jnp.dot(wbuf[n % 2, :, 0:width], turn_values(turn), preferred_element_type=F32)
            acc[span, :] = product if p == 0 else acc[span, :] + product

    for n in range(BLOCKS):
        prepare(wlast.at[n], last, n)
    webuf[:, 0:LAST] = edge_weights(last)
    own_copies[5].wait()
    for d in range(1, BANDS):
        in_copy(d).wait_recv()
    for k in range(*last):
        value_copy(k).wait_recv()

    def edge_copy(n):
        target = ((north, lon), (south, lon), (lat, west), (lat, east))[n]
        landing = (h_out.at[pl.ds(CELLS + SIDE, SIDE)], h_out.at[pl.ds(0, SIDE)], right, left)[n]
        return pltpu.make_async_remote_copy(
            ebuf.at[n], landing, e_send.at[n], e_recv.at[n], device_id=target, device_id_type=MESH)

    def corner_copy(n):
        target = ((north, west), (north, east), (south, west), (south, east))[n]
        return pltpu.make_async_remote_copy(
            cbuf.at[n], corners.at[3 - n], k_send.at[n], k_recv.at[n], device_id=target, device_id_type=MESH)

    @pl.when(always)
    def _():
        inverse = jnp.concatenate(
            [
                recip[0:SIDE, :],
                recip[CELLS - SIDE : CELLS, :],
                recip[pl.ds(0, SIDE, stride=SIDE), :],
                recip[pl.ds(SIDE - 1, SIDE, stride=SIDE), :],
            ],
            axis=0,
        )
        total = eacc[...] + jnp.dot(webuf[:, 0:LAST], turn_values(last), preferred_element_type=F32)
        observed = (total * jnp.concatenate([inverse, inverse], axis=1)).astype(BF16)
        feats = jnp.dot(observed, in_full[...], preferred_element_type=F32)
        ebuf[...] = feats.astype(BF16).reshape(4, SIDE, LATENT)
        for n, at in enumerate((0, SIDE - 1, SIDE, 2 * SIDE - 1)):
            cbuf[n] = jnp.broadcast_to(feats[at : at + 1], (16, LATENT)).astype(BF16)

        for n in range(4):
            edge_copy(n).start()
        for n in range(4):
            corner_copy(n).start()

    for n in range(BLOCKS):
        span = slice(n * BLOCK, n * BLOCK + BLOCK)
        acc[span, :] += jnp.dot(wlast[n], turn_values(last), preferred_element_type=F32)
    for n in range(CELLS // 256):
        span = slice(n * 256, n * 256 + 256)
        inverse = recip[span, :]
        observed = (acc[span, :] * jnp.concatenate([inverse, inverse], axis=1)).astype(BF16)
        for q in range(2):
            h_out[SIDE + n * 256 : SIDE + n * 256 + 256, 256 * q : 256 * q + 256] = jnp.dot(
                observed, in_full[:, 256 * q : 256 * q + 256], preferred_element_type=F32
            ).astype(BF16)

    own_copies[6].wait()
    for k in range(1, TILES):
        cell_copy(k).wait_send()
        value_copy(k).wait_send()
    for d in range(1, BANDS):
        in_copy(d).wait_send()
        mix_copy(d).wait_send()
        mix_copy(d).wait_recv()
    for n in range(LATENT // 128):
        column = jnp.broadcast_to(norm[:, 128 * n : 128 * n + 128], (128, 128)).T
        for m in range(LATENT // 128):
            at = (slice(128 * n, 128 * n + 128), slice(128 * m, 128 * m + 128))
            mix_out[at] = (mix_out[at].astype(F32) * column).astype(BF16)
    for n in range(4):
        edge_copy(n).wait_send()
        edge_copy(n).wait_recv()
        corner_copy(n).wait_send()
        corner_copy(n).wait_recv()

    @pl.when(lat == 0)
    def _():
        h_out[0:SIDE, :] = jnp.zeros((SIDE, LATENT), BF16)
        corners[0:2] = jnp.zeros((2, 16, LATENT), BF16)

    @pl.when(lat == BANDS - 1)
    def _():
        h_out[CELLS + SIDE : CELLS + 2 * SIDE, :] = jnp.zeros((SIDE, LATENT), BF16)
        corners[2:4] = jnp.zeros((2, 16, LATENT), BF16)


def encode(vals, tile, cell, inw, mixw, kern, gain):
    vmem = pl.BlockSpec(memory_space=pltpu.VMEM)
    hbm = pl.BlockSpec(memory_space=pltpu.HBM)
    dma = pltpu.SemaphoreType.DMA
    edge = jax.ShapeDtypeStruct((SIDE, LATENT), BF16)
    return pl.pallas_call(
        encode_kernel,
        out_shape=[
            jax.ShapeDtypeStruct((CELLS + 2 * SIDE, LATENT), BF16),
            edge,
            edge,
            jax.ShapeDtypeStruct((4, 16, LATENT), BF16),
            jax.ShapeDtypeStruct((9, LATENT), F32),
            jax.ShapeDtypeStruct((LATENT, LATENT), BF16),
        ],
        in_specs=[hbm] * 7,
        out_specs=[vmem] * 6,
        scratch_shapes=[
            pltpu.VMEM((OWN, NCH), BF16),
            pltpu.VMEM((1, OWN), jnp.int32),
            pltpu.VMEM((1, OWN), jnp.int32),
            pltpu.VMEM((9, LATENT), F32),
            pltpu.VMEM((1, LATENT), F32),
            pltpu.VMEM((CAP, OWN), BF16),
            pltpu.VMEM((TILES, 8, CAP), F32),
            pltpu.VMEM((TILES, 8, CAP), F32),
            pltpu.VMEM((TILES, CAP, NCH), BF16),
            pltpu.VMEM((TILES, CAP, NCH), BF16),
            pltpu.VMEM((NCH, LATENT), BF16),
        ]
        + [pltpu.VMEM((SIDE, SLOTS), BF16)] * 4
        + [pltpu.VMEM((SIDE, SLOTS), F32)] * 4
        + [
            pltpu.VMEM((SIDE, SIDE), F32),
            pltpu.VMEM((CELLS, 128), F32),
            pltpu.VMEM((2, BLOCK, KDIM), BF16),
            pltpu.VMEM((BLOCKS, BLOCK, LAST), BF16),
            pltpu.VMEM((CELLS, NCH), F32),
            pltpu.VMEM((4 * SIDE, NCH), F32),
            pltpu.VMEM((4 * SIDE, KDIM), BF16),
            pltpu.VMEM((4, SIDE, LATENT), BF16),
            pltpu.VMEM((4, 16, LATENT), BF16),
        ]
        + [dma((TILES,))] * 4
        + [dma((BANDS,))] * 4
        + [dma((4,))] * 4
        + [dma((7,))],
        compiler_params=pltpu.CompilerParams(
            collective_id=0, has_side_effects=True, vmem_limit_bytes=32 * 1024 * 1024
        ),
        name="encode",
    )(vals, tile, cell, inw, mixw, kern, gain)


ROWS = 8
PART = 4
TURNS = SIDE // ROWS
EDGE = 8
CHUNKS = LATENT // 128


def mix_kernel(h, left, right, corners, taps, mix, out, hf, nb, sq):
    i = pl.program_id(0)
    nil = i // TURNS

    def widen(p):
        for l in range(CHUNKS):
            rows = h[pl.ds(pl.multiple_of(p * SIDE, SIDE), SIDE), 128 * l : 128 * l + 128]
            hf[l, p, EDGE : EDGE + SIDE, :] = rows.astype(F32)

    @pl.when(i == 0)
    def _():
        for p in range(ROWS + 2):
            widen(p)
        lf = left[...].astype(F32)
        rt = right[...].astype(F32)
        for l in range(CHUNKS):
            lanes = slice(128 * l, 128 * l + 128)
            for r in range(SIDE):
                hf[l, r + 1, EDGE - 1 : EDGE, :] = lf[r : r + 1, lanes]
                hf[l, r + 1, EDGE + SIDE : EDGE + SIDE + 1, :] = rt[r : r + 1, lanes]
            for n, (r, c) in enumerate(((0, EDGE - 1), (0, EDGE + SIDE), (SIDE + 1, EDGE - 1), (SIDE + 1, EDGE + SIDE))):
                hf[l, r, c : c + 1, :] = corners[n].astype(F32)[0:1, lanes]

    r0 = i * ROWS

    def gather(part):
        for l in range(CHUNKS):
            lanes = slice(128 * l, 128 * l + 128)
            tap = [jnp.broadcast_to(taps[t : t + 1, lanes], (8, 128)) for t in range(9)]
            for cb in range(SIDE // 16):
                halves = []
                for u in range(2):
                    sums = [None] * PART
                    for rr in range(PART + 2):
                        for b in range(3):
                            start = nil + EDGE + 16 * cb + 8 * u + b - 1
                            if b == 1:
                                start = EDGE + 16 * cb + 8 * u
                            seen = hf[l, r0 + PART * part + rr, pl.ds(start, 8), :]
                            for a in range(3):
                                o = rr - a
                                if 0 <= o < PART:
                                    term = seen * tap[3 * a + b]
                                    sums[o] = term if sums[o] is None else sums[o] + term
                    halves.append(sums)
                for o in range(PART):
                    pair = jnp.concatenate([halves[0][o], halves[1][o]], axis=0)
                    at = slice(SIDE * o + 16 * cb, SIDE * o + 16 * cb + 16)
                    nb[part, at, lanes] = pair.astype(BF16)
                    square = pair * pair
                    sq[part, at, :] = square if l == 0 else sq[part, at, :] + square

    def finish(part):
        mean = jnp.sum(sq[part], axis=1, keepdims=True) * (1.0 / LATENT)
        scale = lax.rsqrt(mean + 1e-6) * 0.5
        for q in range(2):
            mixed = jnp.dot(nb[part], mix[:, 256 * q : 256 * q + 256], preferred_element_type=F32)
            for m in range(2):
                l = 2 * q + m
                half = mixed[:, 128 * m : 128 * m + 128] * scale
                base = hf[l, pl.ds(r0 + PART * part + 1, PART), EDGE : EDGE + SIDE, :].reshape(PART * SIDE, 128)
                done = base + (half + half * jnp.tanh(half))
                out[PART * part : PART * part + PART, :, 128 * l : 128 * l + 128] = done.astype(BF16).reshape(PART, SIDE, 128)

    parts = ROWS // PART
    for part in range(parts):
        gather(part)
        if part:
            finish(part - 1)
    finish(parts - 1)

    @pl.when(i < TURNS - 1)
    def _():
        for rr in range(ROWS):
            widen(r0 + ROWS + 2 + rr)


def mix_layer(h, left, right, corners, taps, mix):
    vmem = pl.BlockSpec(memory_space=pltpu.VMEM)
    return pl.pallas_call(
        mix_kernel,
        out_shape=jax.ShapeDtypeStruct((SIDE, SIDE, LATENT), BF16),
        grid=(TURNS,),
        in_specs=[vmem] * 6,
        out_specs=pl.BlockSpec((ROWS, SIDE, LATENT), lambda i: (i, 0, 0)),
        scratch_shapes=[
            pltpu.VMEM((CHUNKS, SIDE + 2, SIDE + 2 * EDGE, 128), F32),
            pltpu.VMEM((ROWS // PART, PART * SIDE, LATENT), BF16),
            pltpu.VMEM((ROWS // PART, PART * SIDE, 128), F32),
        ],
        compiler_params=pltpu.CompilerParams(vmem_limit_bytes=32 * 1024 * 1024),
        name="mix_layer",
    )(h, left, right, corners, taps, mix)


def local(reading_values, reading_tile, reading_cell, in_weight, kernel, norm_gain, mix_weight):
    operands = (
        reading_values,
        reading_tile.reshape(1, OWN),
        reading_cell.reshape(1, OWN),
        in_weight,
        mix_weight,
        kernel,
        norm_gain.reshape(1, LATENT),
    )
    return mix_layer(*encode(*(pltpu.with_memory_space_constraint(x, pltpu.HBM) for x in operands)))


def solution(mesh):
    placed = (
        P(("lat", "lon"), None),
        P(("lat", "lon"), None),
        P(("lat", "lon")),
        P("lat", None),
        P(),
        P(),
        P("lat", None),
    )
    return jax.shard_map(
        local, mesh=mesh, in_specs=placed, out_specs=P("lat", "lon", None), check_vma=False
    )
```

```python
import functools

import jax
import jax.numpy as jnp
from jax import lax
from jax.experimental import pallas as pl
from jax.experimental.pallas import tpu as pltpu
from jax.sharding import PartitionSpec as P

F32 = jnp.float32
BF16 = jnp.bfloat16
MESH = pl.DeviceIdType.MESH

NCH = 256
LATENT = 512
SIDE = 64
OWN = 1024
CAP = 128
TILES = 16
BANDS = 8
GROUP = 4
GROUPS = TILES // GROUP
KDIM = GROUP * CAP
SLOTS = TILES * CAP
EDGE = 8
CHUNKS = LATENT // 128
PASSES = ((0, 4), (4, 8), (8, 12), (12, 14), (14, 16))
LAST = (PASSES[-1][1] - PASSES[-1][0]) * CAP
STEPS = ((0, 0), (2, 2), (2, 1), (1, 2), (2, 3), (3, 2), (2, 0), (0, 2), (1, 1), (3, 3), (1, 3), (3, 1), (1, 0), (0, 1), (3, 0), (0, 3))
BLOCK_ROWS = 16
BLOCK = BLOCK_ROWS * SIDE
BLOCKS = SIDE // BLOCK_ROWS
CELLS = SIDE * SIDE
RINGS = ((6, 0, 0), (5, 1, 3), (4, 4, 4), (3, 5, 5), (0, 6, 6))


def iota(shape, dim):
    return lax.broadcasted_iota(jnp.int32, shape, dim)


def nt_dot(a, b):
    return lax.dot_general(a, b, (((1,), (1,)), ((), ())), preferred_element_type=F32)


def exact_dot(a, b):
    return jnp.dot(a, b, preferred_element_type=F32, precision=lax.Precision.HIGHEST)


def wide(row):
    return jnp.broadcast_to(row, (16, row.shape[1])).astype(BF16)


def encode_kernel(
    vals_in, tile_in, cell_in, inw, mixw, kern_in, gain_in,
    hf, taps, mix_out,
    vals, tile, cell, kern, norm, onehot, cmsg, crecv, sbuf, recv, in_full,
    near_r, near_c, gain_r, gain_c, room_r, room_c, er_f, ec_f,
    counts, recip, wbuf, wlast, acc, eacc, webuf, ebuf, cbuf, up, down, left, right, corners,
    v_send, v_recv, c_send, c_recv, i_send, i_recv, m_send, m_recv, e_send, e_recv, k_send, k_recv,
    l_sem,
):
    lat = lax.axis_index("lat")
    lon = lax.axis_index("lon")
    always = lon < TILES
    east, west = (lon + 1) % TILES, (lon + TILES - 1) % TILES
    north, south = (lat + BANDS - 1) % BANDS, (lat + 1) % BANDS
    lon_x, lon_y = lon // 4, lon % 4

    def partner(k):
        return ((lon_x + STEPS[k][0]) % 4) * 4 + (lon_y + STEPS[k][1]) % 4

    own_copies = []
    for n, (source, landing) in enumerate(
        (
            (tile_in, tile),
            (cell_in, cell),
            (vals_in, vals),
            (kern_in, kern),
            (gain_in, norm),
            (inw, in_full.at[pl.ds(pl.multiple_of(lat * 32, 32), 32)]),
            (mixw, mix_out.at[pl.ds(pl.multiple_of(lat * 64, 64), 64)]),
        )
    ):
        own_copies.append(pltpu.make_async_copy(source, landing, l_sem.at[n]))
        own_copies[n].start()

    barrier = pltpu.get_barrier_semaphore()

    def greet(where):
        pl.semaphore_signal(barrier, inc=1, device_id=where, device_id_type=MESH)

    for k in range(1, TILES):
        greet((lat, partner(k)))
    for d in range(1, BANDS):
        greet(((lat + d) % BANDS, lon))
    for a in (north, south):
        for b in (west, east):
            greet((a, b))

    own_copies[0].wait()
    tid = tile[...]
    belongs = (iota((TILES, OWN), 0) == tid).astype(F32)
    before = (iota((128, 128), 0) < iota((128, 128), 1)).astype(F32).astype(BF16)
    carry = jnp.zeros((TILES, 1), F32)
    ranks = []
    for b in range(OWN // 128):
        part = belongs[:, 128 * b : 128 * b + 128]
        within = jnp.dot(part.astype(BF16), before, preferred_element_type=F32)
        ranks.append(jnp.sum(part * (within + carry), axis=0, keepdims=True))
        carry = carry + jnp.sum(part, axis=1, keepdims=True)
    rank = jnp.concatenate(ranks, axis=1)
    onehot[...] = (iota((CAP, OWN), 0).astype(F32) == rank).astype(F32).astype(BF16)

    own_copies[1].wait()
    rows = (cell[...] >> 6).astype(F32) + 1.0
    cols = (cell[...] & 63).astype(F32) + 1.0
    line = iota((8 * TILES, OWN), 0)
    which = line & 7
    info = jnp.where(which == 0, rows, jnp.where(which == 1, cols, 0.0))
    info = jnp.where((line >> 3) == tid, info, 0.0).astype(BF16)
    cmsg[...] = nt_dot(info, onehot[...]).reshape(TILES, 8, CAP)
    crecv[0] = cmsg[lon]

    pl.semaphore_wait(barrier, TILES - 1 + BANDS - 1 + 4)

    def cell_copy(k):
        return pltpu.make_async_remote_copy(
            cmsg.at[partner(k)], crecv.at[k], c_send.at[k], c_recv.at[k],
            device_id=(lat, partner(k)), device_id_type=MESH)

    def value_copy(k):
        return pltpu.make_async_remote_copy(
            sbuf.at[k], recv.at[k], v_send.at[k], v_recv.at[k],
            device_id=(lat, partner(k)), device_id_type=MESH)

    def in_copy(d):
        return pltpu.make_async_remote_copy(
            inw, in_full.at[pl.ds(pl.multiple_of(lat * 32, 32), 32)], i_send.at[d], i_recv.at[d],
            device_id=((lat + d) % BANDS, lon), device_id_type=MESH)

    def mix_copy(d):
        return pltpu.make_async_remote_copy(
            mixw, mix_out.at[pl.ds(pl.multiple_of(lat * 64, 64), 64)], m_send.at[d], m_recv.at[d],
            device_id=((lat + d) % BANDS, lon), device_id_type=MESH)

    own_copies[2].wait()

    def dispatch(g):
        picks = []
        for j in range(GROUP):
            chosen = wide((tid == partner(GROUP * g + j)).astype(F32))
            picks.append(jnp.concatenate([onehot[16 * i : 16 * i + 16] * chosen for i in range(CAP // 16)], axis=0))
        picked = jnp.dot(jnp.concatenate(picks, axis=0), vals[...], preferred_element_type=F32).astype(BF16)
        for j in range(GROUP):
            k = GROUP * g + j
            if k == 0:
                recv[0] = picked[:CAP]
            else:
                sbuf[k] = picked[CAP * j : CAP * j + CAP]
                value_copy(k).start()

    for g in range(GROUPS):
        pl.when(always)(functools.partial(dispatch, g))
        if g == 0:
            for k in range(1, TILES):
                cell_copy(k).start()
    for d in range(1, BANDS):
        in_copy(d).start()
    for d in range(1, BANDS):
        mix_copy(d).start()

    for k in range(1, TILES):
        cell_copy(k).wait_recv()
    counts[...] = jnp.zeros_like(counts)
    place = iota((SIDE, KDIM), 0).astype(F32)
    for g in range(GROUPS):
        hits = []
        for line, near, gain, room, e_f in (
            (0, near_r, gain_r, room_r, er_f),
            (1, near_c, gain_c, room_c, ec_f),
        ):
            spot = jnp.concatenate([crecv[GROUP * g + j][line : line + 1] for j in range(GROUP)], axis=1)
            spot = jnp.where(spot == 0.0, -100.0, spot - 1.0)
            gap = place - spot
            square = gap * gap
            weight = jnp.exp(square * (-1.0 / 36.0))
            span = slice(KDIM * g, KDIM * g + KDIM)
            near[:, span] = square.astype(BF16)
            gain[:, span] = weight.astype(BF16)
            room[:, span] = 36.0 - square
            e_f[:, span] = weight
            hits.append((square == 0.0).astype(F32).astype(BF16))
        counts[...] += nt_dot(hits[1], hits[0])

    gap = jnp.abs(iota((SIDE, SIDE), 0) - iota((SIDE, SIDE), 1))
    fall = jnp.exp((gap * gap).astype(F32) * (-1.0 / 36.0))
    density = jnp.zeros((SIDE, SIDE), F32)
    for half, least, most in RINGS:
        across = exact_dot(jnp.where(gap <= half, fall, 0.0), counts[...])
        density = density + exact_dot(across, jnp.where((gap >= least) & (gap <= most), fall, 0.0))
    inverse = 1.0 / (density + 1.0)
    for r in range(SIDE):
        recip[SIDE * r : SIDE * r + SIDE, :] = jnp.broadcast_to(inverse[:, r : r + 1], (SIDE, 128))

    own_copies[3].wait()
    own_copies[4].wait()
    taps[...] = kern[...]

    def weigh(room, e_f, near, gain, turn, r):
        span = slice(CAP * turn[0], CAP * turn[1])
        rest = wide(room[r : r + 1, span])
        scale = wide(e_f[r : r + 1, span])
        return [
            jnp.where(near[16 * i : 16 * i + 16, span] <= rest, gain[16 * i : 16 * i + 16, span], jnp.zeros((), BF16)) * scale
            for i in range(SIDE // 16)
        ]

    def turn_values(turn):
        return recv[turn[0] : turn[1]].reshape((turn[1] - turn[0]) * CAP, NCH)

    def edge_weights(turn):
        return jnp.concatenate(
            weigh(room_r, er_f, near_c, gain_c, turn, 0)
            + weigh(room_r, er_f, near_c, gain_c, turn, SIDE - 1)
            + weigh(room_c, ec_f, near_r, gain_r, turn, 0)
            + weigh(room_c, ec_f, near_r, gain_r, turn, SIDE - 1),
            axis=0,
        )

    def prepare(target, turn, n):
        width = (turn[1] - turn[0]) * CAP
        for rr in range(BLOCK_ROWS):
            pieces = weigh(room_r, er_f, near_c, gain_c, turn, n * BLOCK_ROWS + rr)
            target[SIDE * rr : SIDE * rr + SIDE, 0:width] = jnp.concatenate(pieces, axis=0)

    last = PASSES[-1]
    for p, turn in enumerate(PASSES[:-1]):
        width = (turn[1] - turn[0]) * CAP
        webuf[:, 0:width] = edge_weights(turn)
        prepare(wbuf.at[0], turn, 0)
        for k in range(*turn):
            if k:
                value_copy(k).wait_recv()
        product = jnp.dot(webuf[:, 0:width], turn_values(turn), preferred_element_type=F32)
        eacc[...] = product if p == 0 else eacc[...] + product
        for n in range(BLOCKS):
            span = slice(n * BLOCK, n * BLOCK + BLOCK)
            if n + 1 < BLOCKS:
                prepare(wbuf.at[(n + 1) % 2], turn, n + 1)
            product = jnp.dot(wbuf[n % 2, :, 0:width], turn_values(turn), preferred_element_type=F32)
            acc[span, :] = product if p == 0 else acc[span, :] + product

    for n in range(BLOCKS):
        prepare(wlast.at[n], last, n)
    webuf[:, 0:LAST] = edge_weights(last)
    own_copies[5].wait()
    for d in range(1, BANDS):
        in_copy(d).wait_recv()
    for k in range(*last):
        value_copy(k).wait_recv()

    def edge_copy(n):
        target = ((north, lon), (south, lon), (lat, west), (lat, east))[n]
        landing = (down, up, right, left)[n]
        return pltpu.make_async_remote_copy(
            ebuf.at[n], landing, e_send.at[n], e_recv.at[n], device_id=target, device_id_type=MESH)

    def corner_copy(n):
        target = ((north, west), (north, east), (south, west), (south, east))[n]
        return pltpu.make_async_remote_copy(
            cbuf.at[n], corners.at[3 - n], k_send.at[n], k_recv.at[n], device_id=target, device_id_type=MESH)

    @pl.when(always)
    def _():
        inverse = jnp.concatenate(
            [
                recip[0:SIDE, :],
                recip[CELLS - SIDE : CELLS, :],
                recip[pl.ds(0, SIDE, stride=SIDE), :],
                recip[pl.ds(SIDE - 1, SIDE, stride=SIDE), :],
            ],
            axis=0,
        )
        total = eacc[...] + jnp.dot(webuf[:, 0:LAST], turn_values(last), preferred_element_type=F32)
        observed = (total * jnp.concatenate([inverse, inverse], axis=1)).astype(BF16)
        feats = jnp.dot(observed, in_full[...], preferred_element_type=F32)
        ebuf[...] = feats.astype(BF16).reshape(4, SIDE, LATENT)
        for n, at in enumerate((0, SIDE - 1, SIDE, 2 * SIDE - 1)):
            cbuf[n] = jnp.broadcast_to(feats[at : at + 1], (16, LATENT)).astype(BF16)

        for n in range(4):
            corner_copy(n).start()
        for n in range(4):
            edge_copy(n).start()

    for n in range(BLOCKS):
        span = slice(n * BLOCK, n * BLOCK + BLOCK)
        acc[span, :] += jnp.dot(wlast[n], turn_values(last), preferred_element_type=F32)
    for n in range(CELLS // 256):
        span = slice(n * 256, n * 256 + 256)
        inverse = recip[span, :]
        observed = (acc[span, :] * jnp.concatenate([inverse, inverse], axis=1)).astype(BF16)
        for q in range(2):
            feats = jnp.dot(observed, in_full[:, 256 * q : 256 * q + 256], preferred_element_type=F32)
            feats = feats.astype(BF16).astype(F32)
            for m in range(2):
                hf[2 * q + m, 4 * n + 1 : 4 * n + 5, EDGE : EDGE + SIDE, :] = feats[:, 128 * m : 128 * m + 128].reshape(
                    4, SIDE, 128
                )

    own_copies[6].wait()
    for k in range(1, TILES):
        cell_copy(k).wait_send()
        value_copy(k).wait_send()
    for d in range(1, BANDS):
        in_copy(d).wait_send()
        mix_copy(d).wait_send()
        mix_copy(d).wait_recv()
    for n in range(LATENT // 128):
        column = jnp.broadcast_to(norm[:, 128 * n : 128 * n + 128], (128, 128)).T
        for m in range(LATENT // 128):
            at = (slice(128 * n, 128 * n + 128), slice(128 * m, 128 * m + 128))
            mix_out[at] = (mix_out[at].astype(F32) * column).astype(BF16)
    for n in range(4):
        edge_copy(n).wait_send()
        edge_copy(n).wait_recv()
        corner_copy(n).wait_send()
        corner_copy(n).wait_recv()

    above = jnp.where(lat > 0, 1.0, 0.0)
    below = jnp.where(lat < BANDS - 1, 1.0, 0.0)
    lf = left[...].astype(F32)
    rt = right[...].astype(F32)
    for l in range(CHUNKS):
        lanes = slice(128 * l, 128 * l + 128)
        hf[l, 0, EDGE : EDGE + SIDE, :] = up[:, lanes].astype(F32) * above
        hf[l, SIDE + 1, EDGE : EDGE + SIDE, :] = down[:, lanes].astype(F32) * below
        for r in range(SIDE):
            hf[l, r + 1, EDGE - 1 : EDGE, :] = lf[r : r + 1, lanes]
            hf[l, r + 1, EDGE + SIDE : EDGE + SIDE + 1, :] = rt[r : r + 1, lanes]
        for n, (r, c, keep) in enumerate(
            (
                (0, EDGE - 1, above),
                (0, EDGE + SIDE, above),
                (SIDE + 1, EDGE - 1, below),
                (SIDE + 1, EDGE + SIDE, below),
            )
        ):
            hf[l, r, c : c + 1, :] = corners[n].astype(F32)[0:1, lanes] * keep


def encode(vals, tile, cell, inw, mixw, kern, gain):
    vmem = pl.BlockSpec(memory_space=pltpu.VMEM)
    hbm = pl.BlockSpec(memory_space=pltpu.HBM)
    dma = pltpu.SemaphoreType.DMA
    return pl.pallas_call(
        encode_kernel,
        out_shape=[
            jax.ShapeDtypeStruct((CHUNKS, SIDE + 2, SIDE + 2 * EDGE, 128), F32),
            jax.ShapeDtypeStruct((9, LATENT), F32),
            jax.ShapeDtypeStruct((LATENT, LATENT), BF16),
        ],
        in_specs=[hbm] * 7,
        out_specs=[vmem] * 3,
        scratch_shapes=[
            pltpu.VMEM((OWN, NCH), BF16),
            pltpu.VMEM((1, OWN), jnp.int32),
            pltpu.VMEM((1, OWN), jnp.int32),
            pltpu.VMEM((9, LATENT), F32),
            pltpu.VMEM((1, LATENT), F32),
            pltpu.VMEM((CAP, OWN), BF16),
            pltpu.VMEM((TILES, 8, CAP), F32),
            pltpu.VMEM((TILES, 8, CAP), F32),
            pltpu.VMEM((TILES, CAP, NCH), BF16),
            pltpu.VMEM((TILES, CAP, NCH), BF16),
            pltpu.VMEM((NCH, LATENT), BF16),
        ]
        + [pltpu.VMEM((SIDE, SLOTS), BF16)] * 4
        + [pltpu.VMEM((SIDE, SLOTS), F32)] * 4
        + [
            pltpu.VMEM((SIDE, SIDE), F32),
            pltpu.VMEM((CELLS, 128), F32),
            pltpu.VMEM((2, BLOCK, KDIM), BF16),
            pltpu.VMEM((BLOCKS, BLOCK, LAST), BF16),
            pltpu.VMEM((CELLS, NCH), F32),
            pltpu.VMEM((4 * SIDE, NCH), F32),
            pltpu.VMEM((4 * SIDE, KDIM), BF16),
            pltpu.VMEM((4, SIDE, LATENT), BF16),
            pltpu.VMEM((4, 16, LATENT), BF16),
        ]
        + [pltpu.VMEM((SIDE, LATENT), BF16)] * 4
        + [pltpu.VMEM((4, 16, LATENT), BF16)]
        + [dma((TILES,))] * 4
        + [dma((BANDS,))] * 4
        + [dma((4,))] * 4
        + [dma((7,))],
        compiler_params=pltpu.CompilerParams(
            collective_id=0, has_side_effects=True, vmem_limit_bytes=32 * 1024 * 1024
        ),
        name="encode",
    )(vals, tile, cell, inw, mixw, kern, gain)


ROWS = 8
PART = 4
TURNS = SIDE // ROWS


def mix_kernel(hf, taps, mix, out, nb, sq):
    i = pl.program_id(0)
    nil = i // TURNS

    r0 = i * ROWS

    def gather(part):
        for l in range(CHUNKS):
            lanes = slice(128 * l, 128 * l + 128)
            tap = [jnp.broadcast_to(taps[t : t + 1, lanes], (8, 128)) for t in range(9)]
            for cb in range(SIDE // 16):
                halves = []
                for u in range(2):
                    sums = [None] * PART
                    for rr in range(PART + 2):
                        for b in range(3):
                            start = nil + EDGE + 16 * cb + 8 * u + b - 1
                            if b == 1:
                                start = EDGE + 16 * cb + 8 * u
                            seen = hf[l, r0 + PART * part + rr, pl.ds(start, 8), :]
                            for a in range(3):
                                o = rr - a
                                if 0 <= o < PART:
                                    term = seen * tap[3 * a + b]
                                    sums[o] = term if sums[o] is None else sums[o] + term
                    halves.append(sums)
                for o in range(PART):
                    pair = jnp.concatenate([halves[0][o], halves[1][o]], axis=0)
                    at = slice(SIDE * o + 16 * cb, SIDE * o + 16 * cb + 16)
                    nb[part, at, lanes] = pair.astype(BF16)
                    square = pair * pair
                    sq[part, at, :] = square if l == 0 else sq[part, at, :] + square

    def finish(part):
        mean = jnp.sum(sq[part], axis=1, keepdims=True) * (1.0 / LATENT)
        scale = lax.rsqrt(mean + 1e-6) * 0.5
        for q in range(2):
            mixed = jnp.dot(nb[part], mix[:, 256 * q : 256 * q + 256], preferred_element_type=F32)
            for m in range(2):
                l = 2 * q + m
                half = mixed[:, 128 * m : 128 * m + 128] * scale
                base = hf[l, pl.ds(r0 + PART * part + 1, PART), EDGE : EDGE + SIDE, :].reshape(PART * SIDE, 128)
                done = base + (half + half * jnp.tanh(half))
                out[PART * part : PART * part + PART, :, 128 * l : 128 * l + 128] = done.astype(BF16).reshape(PART, SIDE, 128)

    parts = ROWS // PART
    for part in range(parts):
        gather(part)
        if part:
            finish(part - 1)
    finish(parts - 1)


def mix_layer(hf, taps, mix):
    vmem = pl.BlockSpec(memory_space=pltpu.VMEM)
    return pl.pallas_call(
        mix_kernel,
        out_shape=jax.ShapeDtypeStruct((SIDE, SIDE, LATENT), BF16),
        grid=(TURNS,),
        in_specs=[vmem] * 3,
        out_specs=pl.BlockSpec((ROWS, SIDE, LATENT), lambda i: (i, 0, 0)),
        scratch_shapes=[
            pltpu.VMEM((ROWS // PART, PART * SIDE, LATENT), BF16),
            pltpu.VMEM((ROWS // PART, PART * SIDE, 128), F32),
        ],
        compiler_params=pltpu.CompilerParams(vmem_limit_bytes=32 * 1024 * 1024),
        name="mix_layer",
    )(hf, taps, mix)


def local(reading_values, reading_tile, reading_cell, in_weight, kernel, norm_gain, mix_weight):
    operands = (
        reading_values,
        reading_tile.reshape(1, OWN),
        reading_cell.reshape(1, OWN),
        in_weight,
        mix_weight,
        kernel,
        norm_gain.reshape(1, LATENT),
    )
    return mix_layer(*encode(*(pltpu.with_memory_space_constraint(x, pltpu.HBM) for x in operands)))


def solution(mesh):
    placed = (
        P(("lat", "lon"), None),
        P(("lat", "lon"), None),
        P(("lat", "lon")),
        P("lat", None),
        P(),
        P(),
        P("lat", None),
    )
    return jax.shard_map(
        local, mesh=mesh, in_specs=placed, out_specs=P("lat", "lon", None), check_vma=False
    )
```

```python
import functools

import jax
import jax.numpy as jnp
from jax import lax
from jax.experimental import pallas as pl
from jax.experimental.pallas import tpu as pltpu
from jax.sharding import PartitionSpec as P

F32 = jnp.float32
BF16 = jnp.bfloat16
MESH = pl.DeviceIdType.MESH

NCH = 256
LATENT = 512
SIDE = 64
OWN = 1024
CAP = 128
TILES = 16
BANDS = 8
GROUP = 4
GROUPS = TILES // GROUP
KDIM = GROUP * CAP
SLOTS = TILES * CAP
EDGE = 8
CHUNKS = LATENT // 128
PASSES = ((0, 4), (4, 8), (8, 12), (12, 14), (14, 16))
LAST = (PASSES[-1][1] - PASSES[-1][0]) * CAP
STEPS = ((0, 0), (2, 2), (2, 1), (1, 2), (2, 3), (3, 2), (2, 0), (0, 2), (1, 1), (3, 3), (1, 3), (3, 1), (1, 0), (0, 1), (3, 0), (0, 3))
BLOCK_ROWS = 16
BLOCK = BLOCK_ROWS * SIDE
BLOCKS = SIDE // BLOCK_ROWS
CELLS = SIDE * SIDE
RINGS = ((6, 0, 0), (5, 1, 3), (4, 4, 4), (3, 5, 5), (0, 6, 6))


def iota(shape, dim):
    return lax.broadcasted_iota(jnp.int32, shape, dim)


def nt_dot(a, b):
    return lax.dot_general(a, b, (((1,), (1,)), ((), ())), preferred_element_type=F32)


def exact_dot(a, b):
    return jnp.dot(a, b, preferred_element_type=F32, precision=lax.Precision.HIGHEST)


def wide(row):
    return jnp.broadcast_to(row, (16, row.shape[1])).astype(BF16)


def encode_kernel(
    vals_in, tile_in, cell_in, inw, mixw, kern_in, gain_in,
    hf, taps, mix_out,
    vals, tile, cell, kern, norm, onehot, cmsg, crecv, sbuf, recv, in_full,
    near_r, near_c, gain_r, gain_c, room_r, room_c, er_f, ec_f,
    counts, recip, wbuf, wlast, acc, eacc, webuf, ebuf, cbuf, up, down, left, right, corners,
    v_send, v_recv, c_send, c_recv, i_send, i_recv, m_send, m_recv, e_send, e_recv, k_send, k_recv,
    l_sem,
):
    lat = lax.axis_index("lat")
    lon = lax.axis_index("lon")
    always = lon < TILES
    east, west = (lon + 1) % TILES, (lon + TILES - 1) % TILES
    north, south = (lat + BANDS - 1) % BANDS, (lat + 1) % BANDS
    lon_x, lon_y = lon // 4, lon % 4

    def partner(k):
        return ((lon_x + STEPS[k][0]) % 4) * 4 + (lon_y + STEPS[k][1]) % 4

    own_copies = []
    for n, (source, landing) in enumerate(
        (
            (tile_in, tile),
            (cell_in, cell),
            (vals_in, vals),
            (kern_in, kern),
            (gain_in, norm),
            (inw, in_full.at[pl.ds(pl.multiple_of(lat * 32, 32), 32)]),
            (mixw, mix_out.at[pl.ds(pl.multiple_of(lat * 64, 64), 64)]),
        )
    ):
        own_copies.append(pltpu.make_async_copy(source, landing, l_sem.at[n]))
        own_copies[n].start()

    barrier = pltpu.get_barrier_semaphore()

    def greet(where):
        pl.semaphore_signal(barrier, inc=1, device_id=where, device_id_type=MESH)

    for k in range(1, TILES):
        greet((lat, partner(k)))
    for d in range(1, BANDS):
        greet(((lat + d) % BANDS, lon))
    for a in (north, south):
        for b in (west, east):
            greet((a, b))

    own_copies[0].wait()
    tid = tile[...]
    belongs = (iota((TILES, OWN), 0) == tid).astype(F32)
    before = (iota((128, 128), 0) < iota((128, 128), 1)).astype(F32).astype(BF16)
    carry = jnp.zeros((TILES, 1), F32)
    ranks = []
    for b in range(OWN // 128):
        part = belongs[:, 128 * b : 128 * b + 128]
        within = jnp.dot(part.astype(BF16), before, preferred_element_type=F32)
        ranks.append(jnp.sum(part * (within + carry), axis=0, keepdims=True))
        carry = carry + jnp.sum(part, axis=1, keepdims=True)
    rank = jnp.concatenate(ranks, axis=1)
    onehot[...] = (iota((CAP, OWN), 0).astype(F32) == rank).astype(F32).astype(BF16)

    own_copies[1].wait()
    rows = (cell[...] >> 6).astype(F32) + 1.0
    cols = (cell[...] & 63).astype(F32) + 1.0
    line = iota((8 * TILES, OWN), 0)
    which = line & 7
    info = jnp.where(which == 0, rows, jnp.where(which == 1, cols, 0.0))
    info = jnp.where((line >> 3) == tid, info, 0.0).astype(BF16)
    cmsg[...] = nt_dot(info, onehot[...]).reshape(TILES, 8, CAP)
    crecv[0] = cmsg[lon]

    pl.semaphore_wait(barrier, TILES - 1 + BANDS - 1 + 4)

    def cell_copy(k):
        return pltpu.make_async_remote_copy(
            cmsg.at[partner(k)], crecv.at[k], c_send.at[k], c_recv.at[k],
            device_id=(lat, partner(k)), device_id_type=MESH)

    def value_copy(k):
        return pltpu.make_async_remote_copy(
            sbuf.at[k], recv.at[k], v_send.at[k], v_recv.at[k],
            device_id=(lat, partner(k)), device_id_type=MESH)

    def in_copy(d):
        return pltpu.make_async_remote_copy(
            inw, in_full.at[pl.ds(pl.multiple_of(lat * 32, 32), 32)], i_send.at[d], i_recv.at[d],
            device_id=((lat + d) % BANDS, lon), device_id_type=MESH)

    def mix_copy(d):
        return pltpu.make_async_remote_copy(
            mixw, mix_out.at[pl.ds(pl.multiple_of(lat * 64, 64), 64)], m_send.at[d], m_recv.at[d],
            device_id=((lat + d) % BANDS, lon), device_id_type=MESH)

    own_copies[2].wait()

    def dispatch(g):
        picks = []
        for j in range(GROUP):
            chosen = wide((tid == partner(GROUP * g + j)).astype(F32))
            picks.append(jnp.concatenate([onehot[16 * i : 16 * i + 16] * chosen for i in range(CAP // 16)], axis=0))
        picked = jnp.dot(jnp.concatenate(picks, axis=0), vals[...], preferred_element_type=F32).astype(BF16)
        for j in range(GROUP):
            k = GROUP * g + j
            if k == 0:
                recv[0] = picked[:CAP]
            else:
                sbuf[k] = picked[CAP * j : CAP * j + CAP]
                value_copy(k).start()

    for g in range(GROUPS):
        pl.when(always)(functools.partial(dispatch, g))
        if g == 0:
            for k in range(1, TILES):
                cell_copy(k).start()
    for d in range(1, BANDS):
        in_copy(d).start()
    for d in range(1, BANDS):
        mix_copy(d).start()

    for k in range(1, TILES):
        cell_copy(k).wait_recv()
    counts[...] = jnp.zeros_like(counts)
    place = iota((SIDE, KDIM), 0).astype(F32)
    for g in range(GROUPS):
        hits = []
        for line, near, gain, room, e_f in (
            (0, near_r, gain_r, room_r, er_f),
            (1, near_c, gain_c, room_c, ec_f),
        ):
            spot = jnp.concatenate([crecv[GROUP * g + j][line : line + 1] for j in range(GROUP)], axis=1)
            spot = jnp.where(spot == 0.0, -100.0, spot - 1.0)
            gap = place - spot
            square = gap * gap
            weight = jnp.exp(square * (-1.0 / 36.0))
            span = slice(KDIM * g, KDIM * g + KDIM)
            near[:, span] = square.astype(BF16)
            gain[:, span] = weight.astype(BF16)
            room[:, span] = 36.0 - square
            e_f[:, span] = weight
            hits.append((square == 0.0).astype(F32).astype(BF16))
        counts[...] += nt_dot(hits[1], hits[0])

    gap = jnp.abs(iota((SIDE, SIDE), 0) - iota((SIDE, SIDE), 1))
    fall = jnp.exp((gap * gap).astype(F32) * (-1.0 / 36.0))
    density = jnp.zeros((SIDE, SIDE), F32)
    for half, least, most in RINGS:
        across = exact_dot(jnp.where(gap <= half, fall, 0.0), counts[...])
        density = density + exact_dot(across, jnp.where((gap >= least) & (gap <= most), fall, 0.0))
    inverse = 1.0 / (density + 1.0)
    for r in range(SIDE):
        recip[SIDE * r : SIDE * r + SIDE, :] = jnp.broadcast_to(inverse[:, r : r + 1], (SIDE, 128))

    own_copies[3].wait()
    own_copies[4].wait()
    taps[...] = kern[...]

    def weigh(room, e_f, near, gain, turn, r):
        span = slice(CAP * turn[0], CAP * turn[1])
        rest = wide(room[r : r + 1, span])
        scale = wide(e_f[r : r + 1, span])
        return [
            jnp.where(near[16 * i : 16 * i + 16, span] <= rest, gain[16 * i : 16 * i + 16, span], jnp.zeros((), BF16)) * scale
            for i in range(SIDE // 16)
        ]

    def turn_values(turn):
        return recv[turn[0] : turn[1]].reshape((turn[1] - turn[0]) * CAP, NCH)

    def edge_weights(turn):
        return jnp.concatenate(
            weigh(room_r, er_f, near_c, gain_c, turn, 0)
            + weigh(room_r, er_f, near_c, gain_c, turn, SIDE - 1)
            + weigh(room_c, ec_f, near_r, gain_r, turn, 0)
            + weigh(room_c, ec_f, near_r, gain_r, turn, SIDE - 1),
            axis=0,
        )

    def prepare(target, turn, n):
        width = (turn[1] - turn[0]) * CAP
        for rr in range(BLOCK_ROWS):
            pieces = weigh(room_r, er_f, near_c, gain_c, turn, n * BLOCK_ROWS + rr)
            target[SIDE * rr : SIDE * rr + SIDE, 0:width] = jnp.concatenate(pieces, axis=0)

    last = PASSES[-1]
    for p, turn in enumerate(PASSES[:-1]):
        width = (turn[1] - turn[0]) * CAP
        webuf[:, 0:width] = edge_weights(turn)
        prepare(wbuf.at[0], turn, 0)
        for k in range(*turn):
            if k:
                value_copy(k).wait_recv()
        product = jnp.dot(webuf[:, 0:width], turn_values(turn), preferred_element_type=F32)
        eacc[...] = product if p == 0 else eacc[...] + product
        for n in range(BLOCKS):
            span = slice(n * BLOCK, n * BLOCK + BLOCK)
            if n + 1 < BLOCKS:
                prepare(wbuf.at[(n + 1) % 2], turn, n + 1)
            product = jnp.dot(wbuf[n % 2, :, 0:width], turn_values(turn), preferred_element_type=F32)
            acc[span, :] = product if p == 0 else acc[span, :] + product

    for n in range(BLOCKS):
        prepare(wlast.at[n], last, n)
    webuf[:, 0:LAST] = edge_weights(last)
    own_copies[5].wait()
    for d in range(1, BANDS):
        in_copy(d).wait_recv()
    for k in range(*last):
        value_copy(k).wait_recv()

    def edge_copy(n):
        target = ((north, lon), (south, lon), (lat, west), (lat, east))[n]
        landing = (down, up, right, left)[n]
        return pltpu.make_async_remote_copy(
            ebuf.at[n], landing, e_send.at[n], e_recv.at[n], device_id=target, device_id_type=MESH)

    def corner_copy(n):
        target = ((north, west), (north, east), (south, west), (south, east))[n]
        return pltpu.make_async_remote_copy(
            cbuf.at[n], corners.at[3 - n], k_send.at[n], k_recv.at[n], device_id=target, device_id_type=MESH)

    @pl.when(always)
    def _():
        inverse = jnp.concatenate(
            [
                recip[0:SIDE, :],
                recip[CELLS - SIDE : CELLS, :],
                recip[pl.ds(0, SIDE, stride=SIDE), :],
                recip[pl.ds(SIDE - 1, SIDE, stride=SIDE), :],
            ],
            axis=0,
        )
        total = eacc[...] + jnp.dot(webuf[:, 0:LAST], turn_values(last), preferred_element_type=F32)
        observed = (total * jnp.concatenate([inverse, inverse], axis=1)).astype(BF16)
        feats = jnp.dot(observed, in_full[...], preferred_element_type=F32)
        ebuf[...] = feats.astype(BF16).reshape(4, SIDE, LATENT)
        for n, at in enumerate((0, SIDE - 1, SIDE, 2 * SIDE - 1)):
            cbuf[n] = jnp.broadcast_to(feats[at : at + 1], (16, LATENT)).astype(BF16)

        for n in range(4):
            corner_copy(n).start()
        for n in (2, 3, 0, 1):
            edge_copy(n).start()

    for n in range(BLOCKS):
        span = slice(n * BLOCK, n * BLOCK + BLOCK)
        acc[span, :] += jnp.dot(wlast[n], turn_values(last), preferred_element_type=F32)
    for n in range(CELLS // 256):
        span = slice(n * 256, n * 256 + 256)
        inverse = recip[span, :]
        observed = (acc[span, :] * jnp.concatenate([inverse, inverse], axis=1)).astype(BF16)
        for q in range(2):
            feats = jnp.dot(observed, in_full[:, 256 * q : 256 * q + 256], preferred_element_type=F32)
            feats = feats.astype(BF16).astype(F32)
            for m in range(2):
                hf[2 * q + m, 4 * n + 1 : 4 * n + 5, EDGE : EDGE + SIDE, :] = feats[:, 128 * m : 128 * m + 128].reshape(
                    4, SIDE, 128
                )

    own_copies[6].wait()
    for k in range(1, TILES):
        cell_copy(k).wait_send()
        value_copy(k).wait_send()
    for d in range(1, BANDS):
        in_copy(d).wait_send()
        mix_copy(d).wait_send()
        mix_copy(d).wait_recv()
    for n in range(LATENT // 128):
        column = jnp.broadcast_to(norm[:, 128 * n : 128 * n + 128], (128, 128)).T
        for m in range(LATENT // 128):
            at = (slice(128 * n, 128 * n + 128), slice(128 * m, 128 * m + 128))
            mix_out[at] = (mix_out[at].astype(F32) * column).astype(BF16)
    for n in range(4):
        edge_copy(n).wait_send()
        edge_copy(n).wait_recv()
        corner_copy(n).wait_send()
        corner_copy(n).wait_recv()

    above = jnp.where(lat > 0, 1.0, 0.0)
    below = jnp.where(lat < BANDS - 1, 1.0, 0.0)
    lf = left[...].astype(F32)
    rt = right[...].astype(F32)
    for l in range(CHUNKS):
        lanes = slice(128 * l, 128 * l + 128)
        hf[l, 0, EDGE : EDGE + SIDE, :] = up[:, lanes].astype(F32) * above
        hf[l, SIDE + 1, EDGE : EDGE + SIDE, :] = down[:, lanes].astype(F32) * below
        for r in range(SIDE):
            hf[l, r + 1, EDGE - 1 : EDGE, :] = lf[r : r + 1, lanes]
            hf[l, r + 1, EDGE + SIDE : EDGE + SIDE + 1, :] = rt[r : r + 1, lanes]
        for n, (r, c, keep) in enumerate(
            (
                (0, EDGE - 1, above),
                (0, EDGE + SIDE, above),
                (SIDE + 1, EDGE - 1, below),
                (SIDE + 1, EDGE + SIDE, below),
            )
        ):
            hf[l, r, c : c + 1, :] = corners[n].astype(F32)[0:1, lanes] * keep


def encode(vals, tile, cell, inw, mixw, kern, gain):
    vmem = pl.BlockSpec(memory_space=pltpu.VMEM)
    hbm = pl.BlockSpec(memory_space=pltpu.HBM)
    dma = pltpu.SemaphoreType.DMA
    return pl.pallas_call(
        encode_kernel,
        out_shape=[
            jax.ShapeDtypeStruct((CHUNKS, SIDE + 2, SIDE + 2 * EDGE, 128), F32),
            jax.ShapeDtypeStruct((9, LATENT), F32),
            jax.ShapeDtypeStruct((LATENT, LATENT), BF16),
        ],
        in_specs=[hbm] * 7,
        out_specs=[vmem] * 3,
        scratch_shapes=[
            pltpu.VMEM((OWN, NCH), BF16),
            pltpu.VMEM((1, OWN), jnp.int32),
            pltpu.VMEM((1, OWN), jnp.int32),
            pltpu.VMEM((9, LATENT), F32),
            pltpu.VMEM((1, LATENT), F32),
            pltpu.VMEM((CAP, OWN), BF16),
            pltpu.VMEM((TILES, 8, CAP), F32),
            pltpu.VMEM((TILES, 8, CAP), F32),
            pltpu.VMEM((TILES, CAP, NCH), BF16),
            pltpu.VMEM((TILES, CAP, NCH), BF16),
            pltpu.VMEM((NCH, LATENT), BF16),
        ]
        + [pltpu.VMEM((SIDE, SLOTS), BF16)] * 4
        + [pltpu.VMEM((SIDE, SLOTS), F32)] * 4
        + [
            pltpu.VMEM((SIDE, SIDE), F32),
            pltpu.VMEM((CELLS + SIDE, 128), F32),
            pltpu.VMEM((2, BLOCK, KDIM), BF16),
            pltpu.VMEM((BLOCKS, BLOCK, LAST), BF16),
            pltpu.VMEM((CELLS, NCH), F32),
            pltpu.VMEM((4 * SIDE, NCH), F32),
            pltpu.VMEM((4 * SIDE, KDIM), BF16),
            pltpu.VMEM((4, SIDE, LATENT), BF16),
            pltpu.VMEM((4, 16, LATENT), BF16),
        ]
        + [pltpu.VMEM((SIDE, LATENT), BF16)] * 4
        + [pltpu.VMEM((4, 16, LATENT), BF16)]
        + [dma((TILES,))] * 4
        + [dma((BANDS,))] * 4
        + [dma((4,))] * 4
        + [dma((7,))],
        compiler_params=pltpu.CompilerParams(
            collective_id=0, has_side_effects=True, vmem_limit_bytes=32 * 1024 * 1024
        ),
        name="encode",
    )(vals, tile, cell, inw, mixw, kern, gain)


ROWS = 8
PART = 4
TURNS = SIDE // ROWS


def mix_kernel(hf, taps, mix, out, nb, sq):
    i = pl.program_id(0)
    nil = i // TURNS

    r0 = i * ROWS

    def gather(part):
        for l in range(CHUNKS):
            lanes = slice(128 * l, 128 * l + 128)
            tap = [jnp.broadcast_to(taps[t : t + 1, lanes], (8, 128)) for t in range(9)]
            for cb in range(SIDE // 16):
                halves = []
                for u in range(2):
                    sums = [None] * PART
                    for rr in range(PART + 2):
                        for b in range(3):
                            start = nil + EDGE + 16 * cb + 8 * u + b - 1
                            if b == 1:
                                start = EDGE + 16 * cb + 8 * u
                            seen = hf[l, r0 + PART * part + rr, pl.ds(start, 8), :]
                            for a in range(3):
                                o = rr - a
                                if 0 <= o < PART:
                                    term = seen * tap[3 * a + b]
                                    sums[o] = term if sums[o] is None else sums[o] + term
                    halves.append(sums)
                for o in range(PART):
                    pair = jnp.concatenate([halves[0][o], halves[1][o]], axis=0)
                    at = slice(SIDE * o + 16 * cb, SIDE * o + 16 * cb + 16)
                    nb[part, at, lanes] = pair.astype(BF16)
                    square = pair * pair
                    sq[part, at, :] = square if l == 0 else sq[part, at, :] + square

    def finish(part):
        mean = jnp.sum(sq[part], axis=1, keepdims=True) * (1.0 / LATENT)
        scale = lax.rsqrt(mean + 1e-6) * 0.5
        for q in range(2):
            mixed = jnp.dot(nb[part], mix[:, 256 * q : 256 * q + 256], preferred_element_type=F32)
            for m in range(2):
                l = 2 * q + m
                half = mixed[:, 128 * m : 128 * m + 128] * scale
                base = hf[l, pl.ds(r0 + PART * part + 1, PART), EDGE : EDGE + SIDE, :].reshape(PART * SIDE, 128)
                done = base + (half + half * jnp.tanh(half))
                out[PART * part : PART * part + PART, :, 128 * l : 128 * l + 128] = done.astype(BF16).reshape(PART, SIDE, 128)

    parts = ROWS // PART
    for part in range(parts):
        gather(part)
        if part:
            finish(part - 1)
    finish(parts - 1)


def mix_layer(hf, taps, mix):
    vmem = pl.BlockSpec(memory_space=pltpu.VMEM)
    return pl.pallas_call(
        mix_kernel,
        out_shape=jax.ShapeDtypeStruct((SIDE, SIDE, LATENT), BF16),
        grid=(TURNS,),
        in_specs=[vmem] * 3,
        out_specs=pl.BlockSpec((ROWS, SIDE, LATENT), lambda i: (i, 0, 0)),
        scratch_shapes=[
            pltpu.VMEM((ROWS // PART, PART * SIDE, LATENT), BF16),
            pltpu.VMEM((ROWS // PART, PART * SIDE, 128), F32),
        ],
        compiler_params=pltpu.CompilerParams(vmem_limit_bytes=32 * 1024 * 1024),
        name="mix_layer",
    )(hf, taps, mix)


def local(reading_values, reading_tile, reading_cell, in_weight, kernel, norm_gain, mix_weight):
    operands = (
        reading_values,
        reading_tile.reshape(1, OWN),
        reading_cell.reshape(1, OWN),
        in_weight,
        mix_weight,
        kernel,
        norm_gain.reshape(1, LATENT),
    )
    return mix_layer(*encode(*(pltpu.with_memory_space_constraint(x, pltpu.HBM) for x in operands)))


def solution(mesh):
    placed = (
        P(("lat", "lon"), None),
        P(("lat", "lon"), None),
        P(("lat", "lon")),
        P("lat", None),
        P(),
        P(),
        P("lat", None),
    )
    return jax.shard_map(
        local, mesh=mesh, in_specs=placed, out_specs=P("lat", "lon", None), check_vma=False
    )
```
